32 devices in a mesh: section: 2 (over core), dp: 4 (over z), tensor: 4 (over y, x).
Axes of the slice: x: 2, y: 2, z: 4, core: 2. Of those that a mesh axis runs over, the one named last changes fastest.
Arguments:
- token_ids: int32 [8, 1024], P('dp'), may hold values from 0 to 30719
- targets: int32 [8, 1024], P('dp'), may hold values from 0 to 30719
- lengths: int32 [8, 4], P('dp'), may hold values from 1 to 4, 8 in all within a row
- embedding: bfloat16 [30720, 768], P('tensor'), may hold values from -0.25259074 to 0.25259074
- w_qkv: bfloat16 [2, 768, 3, 768], P('section', None, None, 'tensor'), may hold values from -0.21875 to 0.21875
- b_qv: float32 [2, 2, 768], P('section', None, 'tensor'), may hold values from -1.8 to 1.8
- w_out: bfloat16 [2, 768, 768], P('section', 'tensor'), may hold values from -3.5 to 3.5
- w_in: bfloat16 [2, 768, 3072], P('section', None, 'tensor'), may hold values from -0.21875 to 0.21875
- b_in: float32 [2, 3072], P('section', 'tensor'), may hold values from -1.8 to 1.8
- w_down: bfloat16 [2, 3072, 768], P('section', 'tensor'), may hold values from -0.109375 to 0.109375
- norm_gains: float32 [2, 2, 768], P('section'), may hold values from 0.5 to 1.5
- shifts: float32 [2, 4, 768], P('section'), may hold values from -1.8 to 1.8
- mask_logits: float32 [2, 12, 512, 512], P('section', 'tensor'), may hold values from -6 to 6
- mask_noise: float32 [2, 12, 512, 512], P('section', 'tensor'), may hold values from -6 to 6
Outputs:
- hidden_states: float32 [2, 8, 1024, 768], P('section', 'dp', 'tensor')
- grads_in: float32 [2, 8, 1024, 768], P('section', 'dp', 'tensor')
- d_embedding: float32 [30720, 768], P(('tensor', 'section', 'dp'))
- d_w_qkv: float32 [2, 768, 3, 768], P('section', None, None, 'tensor')
- d_b_qv: float32 [2, 2, 768], P('section', None, 'tensor')
- d_w_out: float32 [2, 768, 768], P('section', 'tensor')
- d_w_in: float32 [2, 768, 3072], P('section', None, 'tensor')
- d_b_in: float32 [2, 3072], P('section', 'tensor')
- d_w_down: float32 [2, 3072, 768], P('section', 'tensor')
- d_norm_gains: float32 [2, 2, 768], P('section')
- d_shifts: float32 [2, 4, 768], P('section')
- d_mask_logits: float32 [2, 12, 512, 512], P('section', 'tensor')
The draws below stay inside these ranges and needn't reach their ends.
Inputs may be any that keep to these rules, and one draw needn't show every extreme that they name: Each row gives the lengths, in buckets of 128 tokens, of the 4 sequences of one micro-batch in order; each row sums to 8.
All inputs are finite; a program needn't handle non-finite values.
Results may differ from the reference program's by a relative error of at most 0.02.
The reference program's roundings to bfloat16 on the way count: a program that leaves them out, or rounds other values in their place, can miss the bound.
Values may be sent and summed in bfloat16 or wider, within the bound.
No kernel may reach another device: no remote copies, remote signals or barrier semaphores. Data moves between devices by JAX's collectives and lax.ppermute only.
A program may use at most 448 MiB of HBM per device.

```python
import math
import jax
import jax.numpy as jnp
import numpy as np
from jax import lax

D = 768
HEADS = 12
HEAD_DIM = 64
FF = 3072
MAXLEN = 512
VOCAB = 30720
SLOTS = 4
BUCKET = 128
MB_TOK = 1024
BATCHES = 8
LAYERS = 2


def draw_embedding(key, part):
    key = jax.random.fold_in(key, 11)
    row_frac = jnp.arange(VOCAB, dtype=jnp.float32)[:, None] / VOCAB
    row_scale = 3.0 ** row_frac
    entries = jax.random.truncated_normal(key, -2.3, 2.3, (VOCAB, D), jnp.float32)
    return (entries * row_scale * D ** (-0.5)).astype(jnp.bfloat16)


def plant(values, own_key, low, largest):
    shape = values.shape
    place = [jax.random.randint(jax.random.fold_in(own_key, axis), (), 0, shape[axis]) for axis in range(len(shape))]
    values = values.at[tuple(place)].set(low)
    longest = shape.index(max(shape))
    place[longest] = (place[longest] + 1) % shape[longest]
    return values.at[tuple(place)].set(largest)


def block_scale(stream_key, dims, shards, low, high):
    def one(axis_at, shards_of):
        heights = jax.random.uniform(jax.random.fold_in(jax.random.fold_in(stream_key, 6), axis_at), (shards_of,), jnp.float32, low / len(shards), high / len(shards))
        return jnp.repeat(jnp.exp(heights), dims[axis_at] // shards_of).reshape((-1,) + (1,) * (len(dims) - axis_at - 1))

    level = one(*shards[0])
    for cut in shards[1:]:
        level = level * one(*cut)
    return level


def cumulative_ranks(count, lean):
    weights = [(1 << 20) // math.isqrt(standing ** lean) + 1 for standing in range(1, count + 1)]
    deviation = 1 + sum(weights) // (1 << 30)
    return np.cumsum(np.array([max(1, weight // deviation) for weight in weights]))


def skewed_ids(stream_key, extent, number_of, slope):
    table = cumulative_ranks(number_of, slope)
    pick = jax.random.randint(jax.random.fold_in(stream_key, 1), extent, 0, int(table[number_of - 1]))
    rank = jnp.searchsorted(jnp.asarray(table, jnp.int32), pick, side="right")
    return jax.random.permutation(jax.random.fold_in(stream_key, 2), number_of)[rank].astype(jnp.int32)


def profile(number_of, total, most, lean):
    weights = [(1 << 20) // math.isqrt(grade ** lean) + 1 for grade in range(2, number_of + 1)]
    spare, counts = total - most - (number_of - 1), [1] * (number_of - 1)
    while spare > 0:
        free = [i for i in range(number_of - 1) if counts[i] < most]
        pool, left = sum([weights[i] for i in free]), spare
        for i in free:
            extra = min(most - counts[i], max(1, left * weights[i] // pool), spare)
            counts[i] = counts[i] + extra
            spare = spare - extra
    return np.array([most] + counts)


def ragged(rng, number_of, total, reach, lean):
    if number_of == 2:
        one = jax.random.randint(rng, (), max(1, total - reach), min(reach, total - 1) + 1)
        return jnp.stack([one, total - one])
    sizes = jnp.asarray(profile(number_of, total, reach, lean), jnp.int32)
    pairs = (number_of - 1) // 2
    giver, taker = sizes[1:1 + 2 * pairs:2], sizes[2:2 + 2 * pairs:2]
    room = jnp.minimum(giver - 1, reach - taker)
    shifted = jax.random.randint(jax.random.fold_in(rng, 1), (pairs,), 0, 1 << 20) % (room + 1)
    sizes = sizes.at[1:1 + 2 * pairs:2].set(giver - shifted).at[2:2 + 2 * pairs:2].set(taker + shifted)
    return sizes[jax.random.permutation(jax.random.fold_in(rng, 2), number_of)]


def noise(stream_key, shape, spread, limit, split=(), held_as=jnp.bfloat16):
    values = jax.random.normal(stream_key, shape, jnp.float32) * spread
    if len(split) > 0:
        values = block_scale(stream_key, shape, split, -0.22, 0.18) * values
    return jnp.clip(values, min=-limit, max=limit).astype(held_as)


def setup_inputs(seed: int = 0) -> dict:
    seeds = jax.random.split(jax.random.key(seed), 15)
    return {
        "token_ids": plant(skewed_ids(seeds[0], (BATCHES, MB_TOK), VOCAB, 2), jax.random.fold_in(seeds[0], 3), 0, VOCAB - 1).astype(jnp.int32),
        "targets": plant(skewed_ids(seeds[1], (BATCHES, MB_TOK), VOCAB, 1), jax.random.fold_in(seeds[1], 3), 0, VOCAB - 1).astype(jnp.int32),
        "lengths": jax.vmap(lambda own: ragged(own, SLOTS, 8, 4, 1))(jax.random.split(seeds[2], BATCHES)).reshape((BATCHES, SLOTS)).astype(jnp.int32),
        "embedding": draw_embedding(jax.random.fold_in(seeds[14], 71), 0),
        "w_qkv": noise(seeds[4], (LAYERS, D, 3, D), D ** -0.5, 0.21875, ((0, 2), (3, 4))),
        "b_qv": noise(seeds[5], (LAYERS, 2, D), 0.3, 1.8, ((0, 2), (2, 4)), jnp.float32),
        "w_out": noise(seeds[6], (LAYERS, D, D), 3 ** -0.5, 3.5, ((0, 2), (1, 4))),
        "w_in": noise(seeds[7], (LAYERS, D, FF), D ** -0.5, 0.21875, ((0, 2), (2, 4))),
        "b_in": noise(seeds[8], (LAYERS, FF), 0.3, 1.8, ((0, 2), (1, 4)), jnp.float32),
        "w_down": noise(seeds[9], (LAYERS, FF, D), FF ** -0.5, 0.109375, ((0, 2), (1, 4))),
        "norm_gains": jnp.clip(1.0 + 0.1 * jax.random.normal(seeds[10], (LAYERS, 2, D), jnp.float32), 0.5, 1.5),
        "shifts": noise(seeds[11], (LAYERS, 4, D), 0.3, 1.8, ((0, 2),), jnp.float32),
        "mask_logits": noise(seeds[12], (LAYERS, HEADS, MAXLEN, MAXLEN), 1.0, 6.0, ((0, 2), (1, 4)), jnp.float32),
        "mask_noise": noise(seeds[13], (LAYERS, HEADS, MAXLEN, MAXLEN), 1.0, 6.0, ((0, 2), (1, 4)), jnp.float32),
    }


@jax.custom_vjp
def low(v):
    return lax.optimization_barrier(v.astype(jnp.bfloat16)).astype(jnp.float32)

@jax.custom_vjp
def low_back(v):
    return v

def low_keep(v):
    return (low(v), None)

def low_pass(kept, grad):
    return (grad,)

def back_keep(v):
    return (v, None)

def back_low(kept, grad):
    return (low(grad),)
low.defvjp(low_keep, low_pass)
low_back.defvjp(back_keep, back_low)
EPSILON = 1e-12
LOSS_SCALE = 16.0

def times(left, right):
    return jnp.dot(left, right, precision=lax.Precision.HIGHEST, preferred_element_type=jnp.float32)

def layer_norm(value_in, gain, shift):
    row_mean = lax.optimization_barrier(jnp.mean(value_in, axis=-1, keepdims=True))
    centered = value_in - row_mean
    variance = lax.optimization_barrier(jnp.mean(centered * centered, axis=-1, keepdims=True))
    return centered * lax.rsqrt(variance + EPSILON) * gain + shift

def slot_layout(seq_units):
    seq_lens = seq_units * BUCKET
    starts = jnp.cumsum(seq_lens) - seq_lens
    position = jnp.arange(MAXLEN, dtype=jnp.int32)
    gather_index = jnp.minimum(starts[:, None] + position[None, :], MB_TOK - 1).astype(jnp.int32)
    valid_keys = position[None, :] < seq_lens[:, None]
    token_pos = jnp.arange(MB_TOK, dtype=jnp.int32)
    owner = lax.optimization_barrier(jnp.sum((token_pos[:, None] >= starts[None, :]).astype(jnp.int32), axis=1)) - 1
    owner_hit = owner[:, None] == jnp.arange(seq_units.shape[0], dtype=jnp.int32)[None, :]
    offset = token_pos - lax.optimization_barrier(jnp.sum(jnp.where(owner_hit, starts[None, :], 0), axis=1))
    return (gather_index, valid_keys, (owner * MAXLEN + offset).astype(jnp.int32))

def layer(inputs, seq_units, gate_probs, w_qkv, b_qv, w_out, w_in, b_in, w_down, gains, shifts):
    gather_index, valid_keys, back_index = slot_layout(seq_units)
    token_count = inputs.shape[0]
    projected = times(low(inputs), w_qkv.reshape(D, 3 * D)).reshape(token_count, 3, D)
    qkv_bias = jnp.stack([b_qv[0], jnp.zeros_like(b_qv[0]), b_qv[1]])
    projected = low_back(low(projected + qkv_bias))
    padded = projected[gather_index] * valid_keys[:, :, None, None].astype(jnp.float32)
    padded = padded.reshape(SLOTS, MAXLEN, 3, HEADS, HEAD_DIM)
    queries = padded[:, :, 0]
    key_rows = padded[:, :, 1]
    values = padded[:, :, 2]
    scores = jnp.einsum('sqhe,skhe->shqk', queries, key_rows, precision=lax.Precision.HIGHEST) * HEAD_DIM ** (-0.5)
    scores = low_back(scores)
    scores = jnp.where(valid_keys[:, None, None, :], scores, -1e+30)
    attention = jax.nn.softmax(scores, axis=-1)
    mixed_probs = low(attention * gate_probs[None])
    context = jnp.einsum('shqk,skhe->sqhe', mixed_probs, values, precision=lax.Precision.HIGHEST)
    context = low_back(low(context.reshape(SLOTS * MAXLEN, D)))[back_index]
    attended = low_back(times(context, w_out)) + shifts[0]
    hidden = layer_norm(inputs + attended, gains[0], shifts[1])
    pre_act = low_back(times(low(hidden), w_in) + b_in)
    activated = low(jax.nn.gelu(pre_act, approximate=False))
    feed = low_back(times(activated, w_down)) + shifts[2]
    return layer_norm(hidden + feed, gains[1], shifts[3])

def reference(token_ids, targets, lengths, embedding, w_qkv, b_qv, w_out, w_in, b_in, w_down, norm_gains, shifts, mask_logits, mask_noise):
    batch_count = token_ids.shape[0]
    primals = (embedding.astype(jnp.float32), w_qkv.astype(jnp.float32), b_qv.astype(jnp.float32), w_out.astype(jnp.float32), w_in.astype(jnp.float32), b_in.astype(jnp.float32), w_down.astype(jnp.float32), norm_gains.astype(jnp.float32), shifts.astype(jnp.float32), mask_logits.astype(jnp.float32), jnp.zeros((batch_count, 2, MB_TOK, D), jnp.float32))
    noise_all = mask_noise.astype(jnp.float32)

    def total(embed_all, wq_all, bq_all, wo_all, wi_all, bi_all, wd_all, gain_all, shift_all, logit_all, probes_in):
        gate_all = jax.nn.sigmoid(logit_all + noise_all)

        def one_batch(loss_sum, batch_item):
            id_row, target_row, seq_units, probe_pair = batch_item
            first_in = low_back(embed_all[id_row] * D ** 0.5) + probe_pair[0]
            second_in = layer(first_in, seq_units, gate_all[0], wq_all[0], bq_all[0], wo_all[0], wi_all[0], bi_all[0], wd_all[0], gain_all[0], shift_all[0]) + probe_pair[1]
            final_out = layer(second_in, seq_units, gate_all[1], wq_all[1], bq_all[1], wo_all[1], wi_all[1], bi_all[1], wd_all[1], gain_all[1], shift_all[1])
            logits = low_back(times(low(final_out), embed_all.T))
            picked = jnp.take_along_axis(logits, target_row[:, None], axis=1)[:, 0]
            batch_loss = LOSS_SCALE * jnp.sum(jax.nn.logsumexp(logits, axis=-1) - picked)
            return (loss_sum + batch_loss, jnp.stack([second_in, final_out]))
        loss_sum, hidden_all = lax.scan(jax.checkpoint(one_batch), jnp.zeros((), jnp.float32), (token_ids, targets, lengths, probes_in))
        return (loss_sum, hidden_all)
    loss_sum, pullback, hidden_all = jax.vjp(total, *primals, has_aux=True)
    grads = pullback(jnp.ones((), jnp.float32))
    return (hidden_all.transpose(1, 0, 2, 3), grads[10].transpose(1, 0, 2, 3), grads[0], grads[1], grads[2], grads[3], grads[4], grads[5], grads[6], grads[7], grads[8], grads[9])
```

```python
import functools

import jax
import jax.numpy as jnp
from jax import lax
from jax.experimental import pallas as pl
from jax.experimental.pallas import tpu as pltpu
from jax.sharding import PartitionSpec as P

BUCKET = 128
MAXLEN = 512
EPSILON = 1e-12
LOSS_SCALE = 16.0
BF = jnp.bfloat16
F32 = jnp.float32
MIB = 1 << 20
LANES = 128
HEAD_DIM = 64
VOCAB_STEP = 480
BACK_STEP = 960


def nn(left, right):
    return jnp.dot(left, right, preferred_element_type=F32)


def nt(left, right):
    return lax.dot_general(left, right, (((1,), (1,)), ((), ())), preferred_element_type=F32)


def tn(left, right):
    return lax.dot_general(left, right, (((0,), (0,)), ((), ())), preferred_element_type=F32)


def sds(shape, dtype):
    return jax.ShapeDtypeStruct(shape, dtype)


def whole_specs(count):
    return [pl.BlockSpec(memory_space=pltpu.VMEM)] * count


def scalar_specs(count):
    return [pl.BlockSpec(memory_space=pltpu.SMEM)] * count


def kernel_call(kernel, name, outs, scalars, arrays, scratch=(), flops=0, vmem=32):
    moved = sum(a.size * a.dtype.itemsize for a in arrays)
    moved += sum(jnp.dtype(o.dtype).itemsize * functools.reduce(lambda a, b: a * b, o.shape, 1) for o in outs)
    return pl.pallas_call(
        kernel,
        name=name,
        out_shape=outs,
        in_specs=scalar_specs(len(scalars)) + whole_specs(len(arrays)),
        out_specs=whole_specs(len(outs)),
        scratch_shapes=list(scratch),
        compiler_params=pltpu.CompilerParams(vmem_limit_bytes=vmem * MIB),
        cost_estimate=pl.CostEstimate(flops=flops, bytes_accessed=moved, transcendentals=0),
    )(*scalars, *arrays)


def swap(array, axis, bit):
    count = lax.axis_size(axis)
    return lax.ppermute(array, axis, [(i, i ^ bit) for i in range(count)])


def gather_pieces(own):
    half = own.shape[0] // 2
    near = swap(own, "tensor", 1)
    far = swap(own, "tensor", 2)
    corner_low = swap(near[:half], "tensor", 2)
    corner_high = swap(far[half:], "tensor", 1)
    return [own, near, far, corner_low, corner_high]


def reduce_pieces(near, far, corner_low, corner_high):
    half = near.shape[0] // 2
    low = swap(corner_low, "tensor", 1)
    high = swap(corner_high, "tensor", 2)
    far_sum = jnp.concatenate([(far[:half].astype(F32) + low.astype(F32)).astype(BF), far[half:]])
    near_sum = jnp.concatenate([near[:half], (near[half:].astype(F32) + high.astype(F32)).astype(BF)])
    return swap(near_sum, "tensor", 1), swap(far_sum, "tensor", 2)


def copy_pieces(pieces, target):
    at = 0
    for piece in pieces:
        rows = piece.shape[0]
        target[at : at + rows, :] = piece[...]
        at += rows


def store_block(r, value, own, near, far, corner_low, corner_high):
    half = near.shape[0] // 2
    if r == 0:
        own[...] = value
    elif r == 1:
        near[...] = value.astype(BF)
    elif r == 2:
        far[...] = value.astype(BF)
    else:
        corner_low[...] = value[:half].astype(BF)
        corner_high[...] = value[half:].astype(BF)


def piece_outs(rows, width):
    return [
        sds((rows, width), F32),
        sds((rows, width), BF),
        sds((rows, width), BF),
        sds((rows // 2, width), BF),
        sds((rows // 2, width), BF),
    ]


def sequence_of(bucket, len_ref):
    start, length, total = jnp.int32(0), len_ref[0], jnp.int32(0)
    for i in range(len_ref.shape[0]):
        begun = bucket >= total
        start = jnp.where(begun, total, start)
        length = jnp.where(begun, len_ref[i], length)
        total = total + len_ref[i]
    return start, length


def half_masks():
    lane = lax.broadcasted_iota(jnp.int32, (1, LANES), 1)
    low = (lane < HEAD_DIM).astype(F32)
    return [low.astype(BF), (1.0 - low).astype(BF)], lane < HEAD_DIM


TILES = ((0, (0, 1)), (1, (2,)))
PART = 2 * LANES


def block_rows(me, r, rows):
    return pl.ds(pl.multiple_of((me ^ r) * rows, rows), rows)


def attention_forward(len_ref, me_ref, *refs):
    pieces, refs = refs[:5], refs[5:]
    w_ref, b_ref, g_ref, wo_ref, own, near, far, c_low, c_high, x_rel, proj, ctx_rel, ctx = refs
    me = me_ref[0]
    rows = own.shape[0]
    tokens = proj.shape[0]
    copy_pieces(pieces, x_rel)

    @pl.loop(0, 4)
    def project(r):
        value = nn(x_rel[pl.ds(pl.multiple_of(r * rows, rows), rows), :], w_ref[...]) + b_ref[...]
        proj[block_rows(me, r, rows), :] = value.astype(BF)

    masks, low_lane = half_masks()

    @pl.loop(0, tokens // BUCKET)
    def attend(bucket):
        start, length = sequence_of(bucket, len_ref)
        q_rows = pl.ds(pl.multiple_of(bucket * BUCKET, BUCKET), BUCKET)
        gate_rows = pl.ds(pl.multiple_of((bucket - start) * BUCKET, BUCKET), BUCKET)

        def body(size):
            k_rows = pl.ds(pl.multiple_of(start * BUCKET, BUCKET), size)
            for tile, heads in TILES:
                at = tile * LANES
                q = proj[q_rows, at : at + LANES]
                k = proj[k_rows, PART + at : PART + at + LANES]
                v = proj[k_rows, 2 * PART + at : 2 * PART + at + LANES]
                mixed = []
                for i, head in enumerate(heads):
                    qm = q * masks[i] if len(heads) > 1 else q
                    scores = nt(qm, k) * HEAD_DIM ** (-0.5)
                    powers = jnp.exp(scores - jnp.max(scores, axis=-1, keepdims=True))
                    attention = powers * (1.0 / jnp.sum(powers, axis=-1, keepdims=True))
                    gated = (attention * g_ref[head, gate_rows, 0:size]).astype(BF)
                    mixed.append(nn(gated, v))
                value = jnp.where(low_lane, mixed[0], mixed[1]) if len(heads) > 1 else mixed[0]
                ctx[q_rows, at : at + LANES] = value.astype(BF)

        for buckets in range(1, MAXLEN // BUCKET + 1):
            pl.when(length == buckets)(functools.partial(body, buckets * BUCKET))

    for r in range(4):
        block = ctx[block_rows(me, r, rows), :]
        ctx_rel[r * rows : (r + 1) * rows, :] = block
        store_block(r, nn(block, wo_ref[...]), own, near, far, c_low, c_high)


def attention_backward(len_ref, me_ref, *refs):
    pieces, refs = refs[:5], refs[5:]
    w_ref, g_ref, wo_ref, proj, own, near, far, c_low, c_high, d_rel, dproj_rel, d_bias, d_gate, d_ctx, d_key, d_val, dproj = refs
    me = me_ref[0]
    rows = own.shape[0]
    tokens = proj.shape[0]
    copy_pieces(pieces, d_rel)

    @pl.loop(0, 4)
    def context_grad(r):
        value = nt(d_rel[pl.ds(pl.multiple_of(r * rows, rows), rows), :], wo_ref[...])
        d_ctx[block_rows(me, r, rows), :] = value.astype(BF)

    d_gate[...] = jnp.zeros_like(d_gate)
    d_key[...] = jnp.zeros_like(d_key)
    d_val[...] = jnp.zeros_like(d_val)
    masks, low_lane = half_masks()

    @pl.loop(0, tokens // BUCKET)
    def attend(bucket):
        start, length = sequence_of(bucket, len_ref)
        q_rows = pl.ds(pl.multiple_of(bucket * BUCKET, BUCKET), BUCKET)
        gate_rows = pl.ds(pl.multiple_of((bucket - start) * BUCKET, BUCKET), BUCKET)

        def body(size):
            k_rows = pl.ds(pl.multiple_of(start * BUCKET, BUCKET), size)
            for tile, heads in TILES:
                at = tile * LANES
                q = proj[q_rows, at : at + LANES]
                k = proj[k_rows, PART + at : PART + at + LANES]
                v = proj[k_rows, 2 * PART + at : 2 * PART + at + LANES]
                d_out = d_ctx[q_rows, at : at + LANES]
                d_q = []
                key_sum = val_sum = None
                for i, head in enumerate(heads):
                    qm = q * masks[i] if len(heads) > 1 else q
                    dm = d_out * masks[i] if len(heads) > 1 else d_out
                    scores = nt(qm, k) * HEAD_DIM ** (-0.5)
                    powers = jnp.exp(scores - jnp.max(scores, axis=-1, keepdims=True))
                    attention = powers * (1.0 / jnp.sum(powers, axis=-1, keepdims=True))
                    gate = g_ref[head, gate_rows, 0:size]
                    d_mixed = nt(dm, v)
                    d_gate[head, gate_rows, 0:size] += d_mixed * attention
                    d_prob = d_mixed * gate
                    inner = jnp.sum(d_prob * attention, axis=-1, keepdims=True)
                    d_scores = (attention * (d_prob - inner)).astype(BF)
                    gated = (attention * gate).astype(BF)
                    val = tn(gated, dm)
                    key = tn(d_scores, qm)
                    val_sum = val if val_sum is None else val_sum + val
                    key_sum = key if key_sum is None else key_sum + key
                    d_q.append(nn(d_scores, k))
                value = jnp.where(low_lane, d_q[0], d_q[1]) if len(heads) > 1 else d_q[0]
                dproj[q_rows, at : at + LANES] = (value * HEAD_DIM ** (-0.5)).astype(BF)
                d_key[k_rows, at : at + LANES] += key_sum
                d_val[k_rows, at : at + LANES] += val_sum

        for buckets in range(1, MAXLEN // BUCKET + 1):
            pl.when(length == buckets)(functools.partial(body, buckets * BUCKET))

    dproj[:, PART : 2 * PART] = (d_key[...] * HEAD_DIM ** (-0.5)).astype(BF)
    dproj[:, 2 * PART : 3 * PART] = d_val[...].astype(BF)
    sums = jnp.zeros((1, dproj.shape[1]), F32)
    for r in range(4):
        block = dproj[block_rows(me, r, rows), :]
        dproj_rel[r * rows : (r + 1) * rows, :] = block
        sums = sums + jnp.sum(block.astype(F32), axis=0, keepdims=True)
        store_block(r, nt(block, w_ref[...]), own, near, far, c_low, c_high)
    d_bias[...] = sums


def feed_forward(*refs):
    pieces, refs = refs[:5], refs[5:]
    w_in, b_in, w_down, own, near, far, c_low, c_high, h_rel, act, slope = refs
    rows = own.shape[0]
    copy_pieces(pieces, h_rel)
    for r in range(4):
        at = slice(r * rows, (r + 1) * rows)
        pre = nn(h_rel[at, :], w_in[...]) + b_in[...]
        below = 0.5 * (1.0 + lax.erf(pre * 0.7071067811865476))
        active = (pre * below).astype(BF)
        act[at, :] = active
        slope[at, :] = below + pre * jnp.exp(-0.5 * pre * pre) * 0.3989422804014327
        store_block(r, nn(active, w_down[...]), own, near, far, c_low, c_high)


def feed_backward(*refs):
    pieces, refs = refs[:5], refs[5:]
    w_in, w_down, slope, own, near, far, c_low, c_high, d_rel, d_pre, d_bias = refs
    rows = own.shape[0]
    copy_pieces(pieces, d_rel)
    sums = jnp.zeros((1, d_pre.shape[1]), F32)
    for r in range(4):
        at = slice(r * rows, (r + 1) * rows)
        value = (slope[at, :] * nt(d_rel[at, :], w_down[...])).astype(BF)
        d_pre[at, :] = value
        sums = sums + jnp.sum(value.astype(F32), axis=0, keepdims=True)
        store_block(r, nt(value, w_in[...]), own, near, far, c_low, c_high)
    d_bias[...] = sums


def norm_forward(own, near, far, residual, bias, gain, shift, hidden, hidden_low, normed_ref, scale_ref):
    value = residual[...] + (own[...] + near[...].astype(F32) + far[...].astype(F32)) + bias[...]
    centered = value - jnp.mean(value, axis=-1, keepdims=True)
    scale = lax.rsqrt(jnp.mean(centered * centered, axis=-1, keepdims=True) + EPSILON)
    normed = centered * scale
    out = normed * gain[...] + shift[...]
    hidden[...] = out
    hidden_low[...] = out.astype(BF)
    normed_ref[...] = normed
    scale_ref[...] = scale


def norm_grad(grad, normed, scale, gain, d_sum_ref, d_low_ref, sums_ref):
    scaled = grad * gain
    d_sum = scale * (
        scaled
        - jnp.mean(scaled, axis=-1, keepdims=True)
        - normed * jnp.mean(scaled * normed, axis=-1, keepdims=True)
    )
    d_sum_ref[...] = d_sum
    d_low_ref[...] = d_sum.astype(BF)
    sums_ref[0:1, :] = jnp.sum(grad * normed, axis=0, keepdims=True)
    sums_ref[1:2, :] = jnp.sum(grad, axis=0, keepdims=True)
    sums_ref[2:3, :] = jnp.sum(d_sum, axis=0, keepdims=True)


def norm_backward(own, near, far, residual, normed, scale, gain, d_out, d_sum, d_low, sums):
    grad = residual[...] + (own[...] + near[...].astype(F32) + far[...].astype(F32))
    d_out[...] = grad
    norm_grad(grad, normed[...], scale[...], gain[...], d_sum, d_low, sums)


def merge_head(own, near, far, corner, target_rows, normed, scale, gain, d_sum, d_low, sums, spread_ref):
    width = target_rows.shape[1]
    blocks = [own[...], near[...].astype(F32), far[...].astype(F32), corner[...].astype(F32)]
    spreads = [jnp.sum(block[:, width : width + 3], axis=-1, keepdims=True) for block in blocks]
    top = functools.reduce(jnp.maximum, spreads)
    shares = [jnp.exp(spread - top) for spread in spreads]
    total = functools.reduce(lambda a, b: a + b, shares)
    expected = functools.reduce(
        lambda a, b: a + b, [block[:, :width] * (share / total) for block, share in zip(blocks, shares)]
    )
    grad = LOSS_SCALE * (expected - target_rows[...].astype(F32))
    norm_grad(grad, normed[...], scale[...], gain[...], d_sum, d_low, sums)
    spread = top + jnp.log(total)
    spread_ref[...] = jnp.transpose(jnp.broadcast_to(spread, (spread.shape[0], LANES)))[0:8, :]


def head_forward(*refs):
    pieces, refs = refs[:5], refs[5:]
    e_ref, own, near, far, corner, powers_ref, tops_ref, x_rel, grown, top_ref, total_ref = refs
    step = pl.program_id(0)
    rows = own.shape[0]
    width = x_rel.shape[1]

    @pl.when(step == 0)
    def begin():
        copy_pieces(pieces, x_rel)
        grown[...] = jnp.zeros_like(grown)
        top_ref[...] = jnp.full_like(top_ref, -1e30)
        total_ref[...] = jnp.zeros_like(total_ref)

    for r in range(4):
        at = slice(r * rows, (r + 1) * rows)
        logits = nt(e_ref[...], x_rel[at, :])
        old = top_ref[:, at]
        top = jnp.maximum(old, jnp.max(logits, axis=0, keepdims=True))
        fade = jnp.exp(old - top)
        powers = jnp.exp(logits - top)
        total_ref[:, at] = total_ref[:, at] * fade + jnp.sum(powers, axis=0, keepdims=True)
        top_ref[:, at] = top
        low = powers.astype(BF)
        powers_ref[:, at] = low
        grown[0:width, at] = grown[0:width, at] * fade + tn(e_ref[...], low)
    tops_ref[0] = top_ref[...]

    @pl.when(step == pl.num_programs(0) - 1)
    def end():
        total = total_ref[...]
        spread = top_ref[...] + jnp.log(total)
        first = spread.astype(BF).astype(F32)
        second = (spread - first).astype(BF).astype(F32)
        third = spread - first - second
        tail = [first, second, third, jnp.zeros((LANES - 3, total.shape[1]), F32)]
        grown[width : width + LANES, :] = jnp.concatenate(tail, axis=0)
        share = 1.0 / total
        for r, target in enumerate((own, near, far, corner)):
            at = slice(r * rows, (r + 1) * rows)
            target[:, 0:width] = jnp.transpose(grown[0:width, at] * share[:, at]).astype(target.dtype)
            target[:, width : width + LANES] = jnp.transpose(grown[width : width + LANES, at]).astype(target.dtype)


def head_backward(first_ref, *refs):
    pieces, refs = refs[:5], refs[5:]
    spread_refs, refs = refs[:4], refs[4:]
    powers_ref, tops_ref, hit_ref, out, x_rel, spread = refs
    step = pl.program_id(0)

    @pl.when(step == 0)
    def begin():
        copy_pieces(pieces, x_rel)
        for r, ref in enumerate(spread_refs):
            rows = ref.shape[1]
            spread[:, r * rows : (r + 1) * rows] = ref[0:1, :]

    count = tops_ref.shape[0]
    rows = powers_ref.shape[0] // count
    for i in range(count):
        at = slice(i * rows, (i + 1) * rows)
        scale = LOSS_SCALE * jnp.exp(tops_ref[i] - spread[...])
        index = lax.broadcasted_iota(jnp.int32, (rows, 1), 0) + ((step + first_ref[0]) * count + i) * rows
        hit = jnp.where(index == hit_ref[...], LOSS_SCALE, 0.0)
        grads = powers_ref[at, :].astype(F32) * scale - hit
        out[at, :] = nn(grads.astype(BF), x_rel[...]).astype(BF)


def embed_backward(first_ref, *refs):
    pieces, refs = refs[:5], refs[5:]
    id_ref, so_far, out = refs
    vocab = out.shape[0]
    total = so_far[...]
    index = lax.broadcasted_iota(jnp.int32, (vocab, 1), 0) + first_ref[pl.program_id(0)]
    at = 0
    for piece in pieces:
        ids = id_ref[:, at : at + piece.shape[0]]
        total = total + nn(jnp.where(index == ids, 1.0, 0.0).astype(BF), piece[...])
        at += piece.shape[0]
    out[...] = total


def layer_forward(x, x_low, lens, me, weights):
    w_qkv, b_qkv, w_out, w_in, b_in, w_down, gains, shifts, gates = weights
    rows, width = x.shape
    tokens = 4 * rows
    outs = piece_outs(rows, width) + [sds((tokens, width), BF), sds((tokens, 3 * PART), BF), sds((tokens, PART), BF)]
    *parts, x_rel, proj, ctx_rel = kernel_call(
        attention_forward,
        "attention_forward",
        outs,
        [lens, me],
        gather_pieces(x_low) + [w_qkv, b_qkv, gates, w_out],
        [pltpu.VMEM((tokens, PART), BF)],
        flops=2 * tokens * width * 4 * PART,
    )
    near, far = reduce_pieces(*parts[1:])
    norm_outs = [sds((rows, width), F32), sds((rows, width), BF), sds((rows, width), F32), sds((rows, 1), F32)]
    hidden, hidden_low, normed_one, scale_one = kernel_call(
        norm_forward,
        "first_norm",
        norm_outs,
        [],
        [parts[0], near, far, x, shifts[0:1], gains[0:1], shifts[1:2]],
    )
    units = w_in.shape[1]
    outs = piece_outs(rows, width) + [sds((tokens, width), BF), sds((tokens, units), BF), sds((tokens, units), F32)]
    *parts, h_rel, act, slope = kernel_call(
        feed_forward,
        "feed_forward",
        outs,
        [],
        gather_pieces(hidden_low) + [w_in, b_in, w_down],
        flops=4 * tokens * width * units,
    )
    near, far = reduce_pieces(*parts[1:])
    out, out_low, normed_two, scale_two = kernel_call(
        norm_forward,
        "second_norm",
        norm_outs,
        [],
        [parts[0], near, far, hidden, shifts[2:3], gains[1:2], shifts[3:4]],
    )
    return out, out_low, (x_rel, proj, ctx_rel, h_rel, act, slope, normed_one, scale_one, normed_two, scale_two)


def layer_backward(d_two, d_two_low, lens, me, weights, saved, section, head_width):
    w_qkv, b_qkv, w_out, w_in, b_in, w_down, gains, shifts, gates = weights
    x_rel, proj, ctx_rel, h_rel, act, slope, normed_one, scale_one = saved[:8]
    rows, width = d_two.shape
    tokens = 4 * rows
    units = w_in.shape[1]
    outs = piece_outs(rows, width) + [sds((tokens, width), BF), sds((tokens, units), BF), sds((1, units), F32)]
    *parts, d_rel, d_pre, d_b_in = kernel_call(
        feed_backward,
        "feed_backward",
        outs,
        [],
        gather_pieces(d_two_low) + [w_in, w_down, slope],
        flops=4 * tokens * width * units,
    )
    near, far = reduce_pieces(*parts[1:])
    d_w_down = tn(act, d_rel).astype(BF)
    d_w_in = tn(h_rel, d_pre).astype(BF)
    first = section == 0
    sent = swap(jnp.where(first, d_w_down, d_w_in), "section", 1)
    d_feed = dp_sum(plus(jnp.where(first, d_w_in, d_w_down), sent))
    outs = [sds((rows, width), F32), sds((rows, width), F32), sds((rows, width), BF), sds((8, width), F32)]
    _, d_one, d_one_low, sums = kernel_call(
        norm_backward,
        "first_norm_grad",
        outs,
        [],
        [parts[0], near, far, d_two, normed_one, scale_one, gains[0:1]],
    )
    outs = piece_outs(rows, width) + [
        sds((tokens, width), BF),
        sds((tokens, 3 * PART), BF),
        sds((1, 3 * PART), F32),
        sds(gates.shape, F32),
    ]
    *parts, d_rel, dproj, d_b_qkv, d_gate = kernel_call(
        attention_backward,
        "attention_backward",
        outs,
        [lens, me],
        gather_pieces(d_one_low) + [w_qkv, gates, w_out, proj],
        [
            pltpu.VMEM((tokens, PART), BF),
            pltpu.VMEM((tokens, PART), F32),
            pltpu.VMEM((tokens, PART), F32),
            pltpu.VMEM((tokens, 3 * PART), BF),
        ],
        flops=2 * tokens * width * 4 * PART,
        vmem=40,
    )
    near, far = reduce_pieces(*parts[1:])
    d_w_qkv = tn(x_rel, dproj).astype(BF).reshape(width, 3, PART)[:, :, :head_width].reshape(width, 3 * head_width)
    d_w_out = tn(d_rel, ctx_rel).astype(BF)[:, :head_width]
    d_attn = dp_sum(halves(jnp.concatenate([d_w_qkv, d_w_out], axis=1), section))
    d_gate = dp_sum(halves(d_gate.astype(BF).reshape(-1, d_gate.shape[2]), section))
    return (parts[0], near, far, d_one), (d_feed, d_attn, d_gate), (d_b_qkv, d_b_in, sums)


def head_step(pieces, embedding, target_hits):
    rows, width = pieces[0].shape
    tokens = 4 * rows
    vocab = embedding.shape[0]
    steps = vocab // VOCAB_STEP
    fixed = [pl.BlockSpec(p.shape, lambda i: (0, 0)) for p in pieces]
    wide = width + LANES
    block = pl.BlockSpec((rows, wide), lambda i: (0, 0))
    params = pltpu.CompilerParams(vmem_limit_bytes=48 * MIB)
    own, near, far, corner, powers, tops = pl.pallas_call(
        head_forward,
        name="head_forward",
        grid=(steps,),
        in_specs=fixed + [pl.BlockSpec((VOCAB_STEP, width), lambda i: (i, 0))],
        out_specs=[block] * 4
        + [
            pl.BlockSpec((VOCAB_STEP, tokens), lambda i: (i, 0)),
            pl.BlockSpec((1, 1, tokens), lambda i: (i, 0, 0)),
        ],
        out_shape=[sds((rows, wide), F32)]
        + [sds((rows, wide), BF)] * 3
        + [sds((vocab, tokens), BF), sds((steps, 1, tokens), F32)],
        scratch_shapes=[
            pltpu.VMEM((tokens, width), BF),
            pltpu.VMEM((wide, tokens), F32),
            pltpu.VMEM((1, tokens), F32),
            pltpu.VMEM((1, tokens), F32),
        ],
        compiler_params=params,
        cost_estimate=pl.CostEstimate(
            flops=4 * tokens * vocab * width, bytes_accessed=2 * vocab * (width + tokens), transcendentals=vocab * tokens
        ),
    )(*pieces, embedding)

    def finish(spreads, section):
        half_steps = vocab // 2 // BACK_STEP
        def part(which):
            first = (which * half_steps)[None].astype(jnp.int32)
            fixed_two = [pl.BlockSpec(p.shape, lambda i, f: (0, 0)) for p in pieces]
            return pl.pallas_call(
                head_backward,
                name="head_backward",
                grid_spec=pltpu.PrefetchScalarGridSpec(
                    num_scalar_prefetch=1,
                    grid=(half_steps,),
                    in_specs=fixed_two
                    + [pl.BlockSpec(s.shape, lambda i, f: (0, 0)) for s in spreads]
                    + [
                        pl.BlockSpec((BACK_STEP, tokens), lambda i, f: (i + f[0], 0)),
                        pl.BlockSpec((BACK_STEP // VOCAB_STEP, 1, tokens), lambda i, f: (i + f[0], 0, 0)),
                        pl.BlockSpec((1, tokens), lambda i, f: (0, 0)),
                    ],
                    out_specs=pl.BlockSpec((BACK_STEP, width), lambda i, f: (i, 0)),
                    scratch_shapes=[pltpu.VMEM((tokens, width), BF), pltpu.VMEM((1, tokens), F32)],
                ),
                out_shape=sds((vocab // 2, width), BF),
                compiler_params=params,
                cost_estimate=pl.CostEstimate(
                    flops=tokens * vocab * width, bytes_accessed=vocab * (width + tokens), transcendentals=0
                ),
            )(first, *pieces, *spreads, powers, tops, target_hits)

        sent = part(1 - section)
        kept = part(section)
        return plus(kept, swap(sent, "section", 1))

    return (own, near, far, corner), finish


def embed_grad(pieces, ids, firsts, so_far):
    count, width = so_far.shape
    steps = firsts.shape[0]
    tokens = ids.shape[1]
    part = pl.BlockSpec((count // steps, width), lambda i: (i, 0))
    return pl.pallas_call(
        embed_backward,
        name="embed_backward",
        grid=(steps,),
        in_specs=scalar_specs(1)
        + [pl.BlockSpec(p.shape, lambda i: (0, 0)) for p in pieces]
        + [pl.BlockSpec((1, tokens), lambda i: (0, 0)), part],
        out_specs=part,
        out_shape=sds((count, width), F32),
        input_output_aliases={2 + len(pieces): 0},
        compiler_params=pltpu.CompilerParams(vmem_limit_bytes=32 * MIB),
        cost_estimate=pl.CostEstimate(
            flops=2 * tokens * count * width, bytes_accessed=8 * count * width, transcendentals=0
        ),
    )(firsts, *pieces, ids, so_far)


def pad_parts(array, axis):
    pads = [(0, 0)] * array.ndim
    pads[axis] = (0, PART - array.shape[axis])
    return jnp.pad(array, pads)


def lookup_rows(ids, embedding):
    rows = embedding.shape[0]
    inside = (ids >= 0) & (ids < rows)
    found = jnp.where(inside[:, None], embedding[jnp.clip(ids, 0, rows - 1)], jnp.zeros((), BF))
    count = found.shape[0] // 4
    own, near, far, corner = [found[r * count : (r + 1) * count] for r in range(4)]
    near, far = reduce_pieces(near, far, corner[: count // 2], corner[count // 2 :])
    return own + near + far


def halves(array, section):
    half = array.shape[0] // 2
    mine = lax.dynamic_slice_in_dim(array, section * half, half, 0)
    other = lax.dynamic_slice_in_dim(array, (1 - section) * half, half, 0)
    return (mine.astype(F32) + swap(other, "section", 1).astype(F32)).astype(BF)


def plus(left, right):
    return (left.astype(F32) + right.astype(F32)).astype(BF)


def dp_sum(array):
    if lax.axis_size("dp") != 4:
        return lax.psum(array, "dp")
    z = lax.axis_index("dp")
    inward = plus(array, lax.ppermute(array, "dp", [(0, 1), (3, 2)]))
    total = plus(inward, lax.ppermute(inward, "dp", [(1, 2), (2, 1)]))
    outward = lax.ppermute(total, "dp", [(1, 0), (2, 3)])
    return jnp.where((z == 1) | (z == 2), total, outward)


def sum_everywhere(array):
    for axis in ("tensor", "section", "dp"):
        bit = 1
        while bit < lax.axis_size(axis):
            array = array + swap(array, axis, bit)
            bit *= 2
    return array


def shards(
    token_ids,
    targets,
    lengths,
    embedding,
    w_qkv,
    b_qv,
    w_out,
    w_in,
    b_in,
    w_down,
    norm_gains,
    shifts,
    mask_logits,
    mask_noise,
):
    section = lax.axis_index("section")
    first = section == 0
    place = lax.axis_index("tensor")
    me = place[None].astype(jnp.int32)
    tokens = token_ids.shape[1]
    rows = tokens // lax.axis_size("tensor")
    width = embedding.shape[1]
    vocab_rows = embedding.shape[0]
    vocab_start = place * vocab_rows
    head_width = w_qkv.shape[3]
    order = place ^ jnp.arange(4, dtype=jnp.int32)

    gate_own = jax.nn.sigmoid(mask_logits[0] + mask_noise[0])
    small = jnp.concatenate(
        [
            norm_gains[0],
            shifts[0],
            b_in[0][None],
            jnp.pad(b_qv[0], ((0, 0), (0, width - head_width))),
        ]
    )
    held = (w_qkv[0].reshape(width, 3 * head_width), w_out[0], w_in[0], w_down[0], small, gate_own)
    brought = jax.tree.map(lambda a: swap(a, "section", 1), held)

    def weights_of(layer):
        kept = section == layer
        wq, wo, wi, wd, vec, gates = jax.tree.map(lambda a, b: jnp.where(kept, a, b), held, brought)
        bias = jnp.concatenate(
            [
                vec[7:8, :PART],
                jnp.zeros((1, PART), F32),
                vec[8:9, :PART],
            ],
            axis=1,
        )
        wq = pad_parts(wq.reshape(width, 3, head_width), 2).reshape(width, 3 * PART)
        return (wq, bias, pad_parts(wo, 0), wi, vec[6:7], wd, vec[0:2], vec[2:6], gates)

    layers = [weights_of(0), weights_of(1)]
    lens = lax.dynamic_index_in_dim(lengths, section, 0, keepdims=False)

    def mine(ids):
        row = lax.dynamic_index_in_dim(ids, section, 0, keepdims=False)
        return row.reshape(4, rows)[order].reshape(tokens) - vocab_start

    target_local = mine(targets)
    x = lookup_rows(mine(token_ids), embedding).astype(F32) * width**0.5
    target_rows = lookup_rows(target_local, embedding)
    hidden, hidden_low, saved_first = layer_forward(x, x.astype(BF), lens, me, layers[0])
    final, final_low, saved_last = layer_forward(hidden, hidden_low, lens, me, layers[1])

    pieces = gather_pieces(final_low)
    parts, finish_head = head_step(pieces, embedding, target_local[None])
    own, near, far, corner = parts
    outs = [sds((rows, width), F32), sds((rows, width), BF), sds((8, width), F32), sds((8, rows), F32)]
    d_two, d_two_low, sums_two_last, spread = kernel_call(
        merge_head,
        "merge_head",
        outs,
        [],
        [own, swap(near, "tensor", 1), swap(far, "tensor", 2), swap(corner, "tensor", 3), target_rows]
        + [saved_last[8], saved_last[9], layers[1][6][1:2]],
    )
    spreads = [spread] + [swap(spread, "tensor", bit) for bit in (1, 2, 3)]
    d_head = finish_head(spreads, section)
    half_vocab = vocab_rows // 2
    d_head = lax.psum_scatter(d_head, "dp", scatter_dimension=0, tiled=True)

    d_x, grads_last, vecs_last = layer_backward(d_two, d_two_low, lens, me, layers[1], saved_last, section, head_width)
    outs = [sds((rows, width), F32), sds((rows, width), F32), sds((rows, width), BF), sds((8, width), F32)]
    grad_last, d_two, d_two_low, sums_two_first = kernel_call(
        norm_backward,
        "second_norm_grad",
        outs,
        [],
        list(d_x) + [saved_first[8], saved_first[9], layers[0][6][1:2]],
    )
    d_x, grads_first, vecs_first = layer_backward(d_two, d_two_low, lens, me, layers[0], saved_first, section, head_width)
    grad_first = d_x[3] + (d_x[0] + d_x[1].astype(F32) + d_x[2].astype(F32))

    dp = lax.axis_size("dp")
    share = half_vocab // dp
    firsts = lax.axis_index("dp") * share + jnp.arange(2, dtype=jnp.int32) * half_vocab
    rows_here, d_head = lax.optimization_barrier((grad_first.astype(BF), d_head))
    ids_here = mine(token_ids)[None] + vocab_start
    d_rows = jnp.zeros((2 * share, width), F32)
    for other in range(dp):
        ids = ids_here if other == 0 else swap(ids_here, "dp", other)
        rows_there = rows_here if other == 0 else swap(rows_here, "dp", other)
        d_rows = embed_grad(gather_pieces(rows_there), ids - vocab_start, firsts, d_rows)
    kept = lax.dynamic_slice_in_dim(d_rows, section * share, share, 0)
    sent = lax.dynamic_slice_in_dim(d_rows, (1 - section) * share, share, 0).astype(BF)
    d_embedding = d_head.astype(F32) + width**0.5 * (kept + swap(sent, "section", 1).astype(F32))

    def vec_rows(vecs, sums_two):
        d_b_qkv, d_b_in, sums_one = vecs
        wide = jnp.concatenate([sums_one[0:1], sums_two[0:1], sums_one[2:3], sums_one[1:2], sums_two[2:3], sums_two[1:2]])
        narrow = jnp.concatenate(
            [jnp.pad(d_b_qkv[:, :PART], ((0, 0), (0, width - PART))), jnp.pad(d_b_qkv[:, 2 * PART :], ((0, 0), (0, width - PART))), d_b_in]
        )
        spread_out = jnp.where((jnp.arange(4) == place)[:, None, None], narrow[None], 0.0).reshape(12, width)
        return jnp.concatenate([wide, spread_out])

    vecs = jnp.stack([vec_rows(vecs_first, sums_two_first), vec_rows(vecs_last, sums_two_last)])
    vecs = sum_everywhere(vecs)
    vecs = lax.dynamic_index_in_dim(vecs, section, 0, keepdims=False)
    narrow = lax.dynamic_slice_in_dim(vecs, 6 + 3 * place, 3, 0)

    def assembled(low_layer, high_layer):
        got = swap(jnp.where(first, high_layer, low_layer), "section", 1)
        return jnp.where(first, low_layer, got).astype(F32), jnp.where(first, got, high_layer).astype(F32)

    (g_in, g_down), attn, gate = jax.tree.map(assembled, grads_first, grads_last)
    attn = jnp.concatenate(attn)
    g_qkv = attn[:, : 3 * head_width].reshape(width, 3, head_width)
    g_out = attn[:, 3 * head_width :].T
    g_mask = jnp.concatenate(gate).reshape(gate_own.shape) * gate_own * (1.0 - gate_own)

    def placed_rows(low_layer, high_layer):
        got = swap(jnp.where(first, high_layer, low_layer), "section", 1)
        return jnp.where(first, jnp.stack([low_layer, got]), jnp.stack([got, high_layer]))

    return (
        placed_rows(hidden, final)[None],
        placed_rows(grad_first, grad_last)[None],
        d_embedding,
        g_qkv[None],
        narrow[None, 0:2, :head_width],
        g_out[None],
        g_in[None],
        narrow[None, 2],
        g_down[None],
        vecs[None, 0:2],
        vecs[None, 2:6],
        g_mask[None],
    )


def solution(mesh):
    placed = (
        P("dp", None),
        P("dp", None),
        P("dp", None),
        P("tensor", None),
        P("section", None, None, "tensor"),
        P("section", None, "tensor"),
        P("section", "tensor", None),
        P("section", None, "tensor"),
        P("section", "tensor"),
        P("section", "tensor", None),
        P("section", None, None),
        P("section", None, None),
        P("section", "tensor", None, None),
        P("section", "tensor", None, None),
    )
    return jax.shard_map(
        shards,
        mesh=mesh,
        in_specs=placed,
        out_specs=(
            P("section", "dp", "tensor", None),
            P("section", "dp", "tensor", None),
            P(("tensor", "section", "dp"), None),
            P("section", None, None, "tensor"),
            P("section", None, "tensor"),
            P("section", "tensor", None),
            P("section", None, "tensor"),
            P("section", "tensor"),
            P("section", "tensor", None),
            P("section", None, None),
            P("section", None, None),
            P("section", "tensor", None, None),
        ),
        check_vma=False,
    )
```

```python
import functools

import jax
import jax.numpy as jnp
from jax import lax
from jax.experimental import pallas as pl
from jax.experimental.pallas import tpu as pltpu
from jax.sharding import PartitionSpec as P

BUCKET = 128
MAXLEN = 512
EPSILON = 1e-12
LOSS_SCALE = 16.0
BF = jnp.bfloat16
F32 = jnp.float32
MIB = 1 << 20
LANES = 128
HEAD_DIM = 64
VOCAB_STEP = 1536
HEAD_CHUNK = 256


def nn(left, right):
    return jnp.dot(left, right, preferred_element_type=F32)


def nt(left, right):
    return lax.dot_general(left, right, (((1,), (1,)), ((), ())), preferred_element_type=F32)


def tn(left, right):
    return lax.dot_general(left, right, (((0,), (0,)), ((), ())), preferred_element_type=F32)


def sds(shape, dtype):
    return jax.ShapeDtypeStruct(shape, dtype)


def whole_specs(count):
    return [pl.BlockSpec(memory_space=pltpu.VMEM)] * count


def scalar_specs(count):
    return [pl.BlockSpec(memory_space=pltpu.SMEM)] * count


def kernel_call(kernel, name, outs, scalars, arrays, scratch=(), flops=0, vmem=32):
    moved = sum(a.size * a.dtype.itemsize for a in arrays)
    moved += sum(jnp.dtype(o.dtype).itemsize * functools.reduce(lambda a, b: a * b, o.shape, 1) for o in outs)
    return pl.pallas_call(
        kernel,
        name=name,
        out_shape=outs,
        in_specs=scalar_specs(len(scalars)) + whole_specs(len(arrays)),
        out_specs=whole_specs(len(outs)),
        scratch_shapes=list(scratch),
        compiler_params=pltpu.CompilerParams(vmem_limit_bytes=vmem * MIB),
        cost_estimate=pl.CostEstimate(flops=flops, bytes_accessed=moved, transcendentals=0),
    )(*scalars, *arrays)


def swap(array, axis, bit):
    count = lax.axis_size(axis)
    return lax.ppermute(array, axis, [(i, i ^ bit) for i in range(count)])


def gather_pieces(own):
    half = own.shape[0] // 2
    near = swap(own, "tensor", 1)
    far = swap(own, "tensor", 2)
    corner_low = swap(near[:half], "tensor", 2)
    corner_high = swap(far[half:], "tensor", 1)
    return [own, near, far, corner_low, corner_high]


def reduce_pieces(near, far, corner_low, corner_high):
    half = near.shape[0] // 2
    low = swap(corner_low, "tensor", 1)
    high = swap(corner_high, "tensor", 2)
    far_sum = jnp.concatenate([(far[:half].astype(F32) + low.astype(F32)).astype(BF), far[half:]])
    near_sum = jnp.concatenate([near[:half], (near[half:].astype(F32) + high.astype(F32)).astype(BF)])
    return swap(near_sum, "tensor", 1), swap(far_sum, "tensor", 2)


def copy_pieces(pieces, target):
    at = 0
    for piece in pieces:
        rows = piece.shape[0]
        target[at : at + rows, :] = piece[...]
        at += rows


def store_block(r, value, own, near, far, corner_low, corner_high):
    half = near.shape[0] // 2
    if r == 0:
        own[...] = value
    elif r == 1:
        near[...] = value.astype(BF)
    elif r == 2:
        far[...] = value.astype(BF)
    else:
        corner_low[...] = value[:half].astype(BF)
        corner_high[...] = value[half:].astype(BF)


def piece_outs(rows, width):
    return [
        sds((rows, width), F32),
        sds((rows, width), BF),
        sds((rows, width), BF),
        sds((rows // 2, width), BF),
        sds((rows // 2, width), BF),
    ]


def sequence_of(bucket, len_ref):
    start, length, total = jnp.int32(0), len_ref[0], jnp.int32(0)
    for i in range(len_ref.shape[0]):
        begun = bucket >= total
        start = jnp.where(begun, total, start)
        length = jnp.where(begun, len_ref[i], length)
        total = total + len_ref[i]
    return start, length


def half_masks():
    lane = lax.broadcasted_iota(jnp.int32, (1, LANES), 1)
    low = (lane < HEAD_DIM).astype(F32)
    return [low.astype(BF), (1.0 - low).astype(BF)], lane < HEAD_DIM


TILES = ((0, (0, 1)), (1, (2,)))
PART = 2 * LANES


def block_rows(me, r, rows):
    return pl.ds(pl.multiple_of((me ^ r) * rows, rows), rows)


def attention_forward(len_ref, me_ref, *refs):
    pieces, refs = refs[:5], refs[5:]
    w_ref, b_ref, g_ref, wo_ref, own, near, far, c_low, c_high, x_rel, proj, ctx_rel, ctx = refs
    me = me_ref[0]
    rows = own.shape[0]
    tokens = proj.shape[0]
    copy_pieces(pieces, x_rel)

    @pl.loop(0, 4)
    def project(r):
        value = nn(x_rel[pl.ds(pl.multiple_of(r * rows, rows), rows), :], w_ref[...]) + b_ref[...]
        proj[block_rows(me, r, rows), :] = value.astype(BF)

    masks, low_lane = half_masks()

    @pl.loop(0, tokens // BUCKET)
    def attend(bucket):
        start, length = sequence_of(bucket, len_ref)
        q_rows = pl.ds(pl.multiple_of(bucket * BUCKET, BUCKET), BUCKET)
        gate_rows = pl.ds(pl.multiple_of((bucket - start) * BUCKET, BUCKET), BUCKET)

        def body(size):
            k_rows = pl.ds(pl.multiple_of(start * BUCKET, BUCKET), size)
            for tile, heads in TILES:
                at = tile * LANES
                q = proj[q_rows, at : at + LANES]
                k = proj[k_rows, PART + at : PART + at + LANES]
                v = proj[k_rows, 2 * PART + at : 2 * PART + at + LANES]
                mixed = []
                for i, head in enumerate(heads):
                    qm = q * masks[i] if len(heads) > 1 else q
                    scores = nt(qm, k) * HEAD_DIM ** (-0.5)
                    powers = jnp.exp(scores - jnp.max(scores, axis=-1, keepdims=True))
                    attention = powers * (1.0 / jnp.sum(powers, axis=-1, keepdims=True))
                    gated = (attention * g_ref[head, gate_rows, 0:size]).astype(BF)
                    mixed.append(nn(gated, v))
                value = jnp.where(low_lane, mixed[0], mixed[1]) if len(heads) > 1 else mixed[0]
                ctx[q_rows, at : at + LANES] = value.astype(BF)

        for buckets in range(1, MAXLEN // BUCKET + 1):
            pl.when(length == buckets)(functools.partial(body, buckets * BUCKET))

    for r in range(4):
        block = ctx[block_rows(me, r, rows), :]
        ctx_rel[r * rows : (r + 1) * rows, :] = block
        store_block(r, nn(block, wo_ref[...]), own, near, far, c_low, c_high)


def attention_backward(len_ref, me_ref, *refs):
    pieces, refs = refs[:5], refs[5:]
    w_ref, g_ref, wo_ref, proj, own, near, far, c_low, c_high, d_rel, dproj_rel, d_bias, d_gate, d_ctx, d_key, d_val, dproj = refs
    me = me_ref[0]
    rows = own.shape[0]
    tokens = proj.shape[0]
    copy_pieces(pieces, d_rel)

    @pl.loop(0, 4)
    def context_grad(r):
        value = nt(d_rel[pl.ds(pl.multiple_of(r * rows, rows), rows), :], wo_ref[...])
        d_ctx[block_rows(me, r, rows), :] = value.astype(BF)

    d_gate[...] = jnp.zeros_like(d_gate)
    d_key[...] = jnp.zeros_like(d_key)
    d_val[...] = jnp.zeros_like(d_val)
    masks, low_lane = half_masks()

    @pl.loop(0, tokens // BUCKET)
    def attend(bucket):
        start, length = sequence_of(bucket, len_ref)
        q_rows = pl.ds(pl.multiple_of(bucket * BUCKET, BUCKET), BUCKET)
        gate_rows = pl.ds(pl.multiple_of((bucket - start) * BUCKET, BUCKET), BUCKET)

        def body(size):
            k_rows = pl.ds(pl.multiple_of(start * BUCKET, BUCKET), size)
            for tile, heads in TILES:
                at = tile * LANES
                q = proj[q_rows, at : at + LANES]
                k = proj[k_rows, PART + at : PART + at + LANES]
                v = proj[k_rows, 2 * PART + at : 2 * PART + at + LANES]
                d_out = d_ctx[q_rows, at : at + LANES]
                d_q = []
                key_sum = val_sum = None
                for i, head in enumerate(heads):
                    qm = q * masks[i] if len(heads) > 1 else q
                    dm = d_out * masks[i] if len(heads) > 1 else d_out
                    scores = nt(qm, k) * HEAD_DIM ** (-0.5)
                    powers = jnp.exp(scores - jnp.max(scores, axis=-1, keepdims=True))
                    attention = powers * (1.0 / jnp.sum(powers, axis=-1, keepdims=True))
                    gate = g_ref[head, gate_rows, 0:size]
                    d_mixed = nt(dm, v)
                    d_gate[head, gate_rows, 0:size] += d_mixed * attention
                    d_prob = d_mixed * gate
                    inner = jnp.sum(d_prob * attention, axis=-1, keepdims=True)
                    d_scores = (attention * (d_prob - inner)).astype(BF)
                    gated = (attention * gate).astype(BF)
                    val = tn(gated, dm)
                    key = tn(d_scores, qm)
                    val_sum = val if val_sum is None else val_sum + val
                    key_sum = key if key_sum is None else key_sum + key
                    d_q.append(nn(d_scores, k))
                value = jnp.where(low_lane, d_q[0], d_q[1]) if len(heads) > 1 else d_q[0]
                dproj[q_rows, at : at + LANES] = (value * HEAD_DIM ** (-0.5)).astype(BF)
                d_key[k_rows, at : at + LANES] += key_sum
                d_val[k_rows, at : at + LANES] += val_sum

        for buckets in range(1, MAXLEN // BUCKET + 1):
            pl.when(length == buckets)(functools.partial(body, buckets * BUCKET))

    dproj[:, PART : 2 * PART] = (d_key[...] * HEAD_DIM ** (-0.5)).astype(BF)
    dproj[:, 2 * PART : 3 * PART] = d_val[...].astype(BF)
    sums = jnp.zeros((1, dproj.shape[1]), F32)
    for r in range(4):
        block = dproj[block_rows(me, r, rows), :]
        dproj_rel[r * rows : (r + 1) * rows, :] = block
        sums = sums + jnp.sum(block.astype(F32), axis=0, keepdims=True)
        store_block(r, nt(block, w_ref[...]), own, near, far, c_low, c_high)
    d_bias[...] = sums


def feed_forward(*refs):
    pieces, refs = refs[:5], refs[5:]
    w_in, b_in, w_down, own, near, far, c_low, c_high, h_rel, act, slope = refs
    rows = own.shape[0]
    copy_pieces(pieces, h_rel)
    for r in range(4):
        at = slice(r * rows, (r + 1) * rows)
        pre = nn(h_rel[at, :], w_in[...]) + b_in[...]
        below = 0.5 * (1.0 + lax.erf(pre * 0.7071067811865476))
        active = (pre * below).astype(BF)
        act[at, :] = active
        slope[at, :] = below + pre * jnp.exp(-0.5 * pre * pre) * 0.3989422804014327
        store_block(r, nn(active, w_down[...]), own, near, far, c_low, c_high)


def feed_backward(*refs):
    pieces, refs = refs[:5], refs[5:]
    w_in, w_down, slope, own, near, far, c_low, c_high, d_rel, d_pre, d_bias = refs
    rows = own.shape[0]
    copy_pieces(pieces, d_rel)
    sums = jnp.zeros((1, d_pre.shape[1]), F32)
    for r in range(4):
        at = slice(r * rows, (r + 1) * rows)
        value = (slope[at, :] * nt(d_rel[at, :], w_down[...])).astype(BF)
        d_pre[at, :] = value
        sums = sums + jnp.sum(value.astype(F32), axis=0, keepdims=True)
        store_block(r, nt(value, w_in[...]), own, near, far, c_low, c_high)
    d_bias[...] = sums


def norm_forward(own, near, far, residual, bias, gain, shift, hidden, hidden_low, normed_ref, scale_ref):
    value = residual[...] + (own[...] + near[...].astype(F32) + far[...].astype(F32)) + bias[...]
    centered = value - jnp.mean(value, axis=-1, keepdims=True)
    scale = lax.rsqrt(jnp.mean(centered * centered, axis=-1, keepdims=True) + EPSILON)
    normed = centered * scale
    out = normed * gain[...] + shift[...]
    hidden[...] = out
    hidden_low[...] = out.astype(BF)
    normed_ref[...] = normed
    scale_ref[...] = scale


def norm_grad(grad, normed, scale, gain, d_sum_ref, d_low_ref, sums_ref):
    scaled = grad * gain
    d_sum = scale * (
        scaled
        - jnp.mean(scaled, axis=-1, keepdims=True)
        - normed * jnp.mean(scaled * normed, axis=-1, keepdims=True)
    )
    d_sum_ref[...] = d_sum
    d_low_ref[...] = d_sum.astype(BF)
    sums_ref[0:1, :] = jnp.sum(grad * normed, axis=0, keepdims=True)
    sums_ref[1:2, :] = jnp.sum(grad, axis=0, keepdims=True)
    sums_ref[2:3, :] = jnp.sum(d_sum, axis=0, keepdims=True)


def norm_backward(own, near, far, residual, normed, scale, gain, d_out, d_sum, d_low, sums):
    grad = residual[...] + (own[...] + near[...].astype(F32) + far[...].astype(F32))
    d_out[...] = grad
    norm_grad(grad, normed[...], scale[...], gain[...], d_sum, d_low, sums)


def merge_head(own, near, far, corner, target_rows, normed, scale, gain, d_sum, d_low, sums, spread_ref):
    width = target_rows.shape[1]
    blocks = [own[...], near[...].astype(F32), far[...].astype(F32), corner[...].astype(F32)]
    spreads = [jnp.sum(block[:, width : width + 3], axis=-1, keepdims=True) for block in blocks]
    top = functools.reduce(jnp.maximum, spreads)
    shares = [jnp.exp(spread - top) for spread in spreads]
    total = functools.reduce(lambda a, b: a + b, shares)
    expected = functools.reduce(
        lambda a, b: a + b, [block[:, :width] * (share / total) for block, share in zip(blocks, shares)]
    )
    grad = LOSS_SCALE * (expected - target_rows[...].astype(F32))
    norm_grad(grad, normed[...], scale[...], gain[...], d_sum, d_low, sums)
    spread = top + jnp.log(total)
    spread_ref[...] = jnp.transpose(jnp.broadcast_to(spread, (spread.shape[0], LANES)))[0:8, :]


def head_forward(count, *refs):
    pieces, refs = refs[:count], refs[count:]
    e_ref, *outs = refs[:-4]
    x_rel, grown, top_ref, total_ref = refs[-4:]
    step = pl.program_id(0)
    tokens, width = x_rel.shape
    chunks = [slice(at, at + HEAD_CHUNK) for at in range(0, tokens, HEAD_CHUNK)]

    @pl.when(step == 0)
    def begin():
        copy_pieces(pieces, x_rel)
        grown[...] = jnp.zeros_like(grown)
        top_ref[...] = jnp.full_like(top_ref, -1e30)
        total_ref[...] = jnp.zeros_like(total_ref)

    logits = [nt(x_rel[at, :], e_ref[...]) for at in chunks]
    shares = []
    for at, block in zip(chunks, logits):
        old = top_ref[at, :]
        top = jnp.maximum(old, jnp.max(block, axis=1, keepdims=True))
        fade = jnp.exp(old - top)
        powers = jnp.exp(block - top)
        total_ref[at, :] = total_ref[at, :] * fade + jnp.sum(powers, axis=1, keepdims=True)
        top_ref[at, :] = top
        shares.append((fade, powers.astype(BF)))
    for at, (fade, powers) in zip(chunks, shares):
        grown[at, :] = grown[at, :] * fade + nn(powers, e_ref[...])

    @pl.when(step == pl.num_programs(0) - 1)
    def end():
        first_row = 0
        for out in outs:
            rows = out.shape[0]
            at = slice(first_row, first_row + rows)
            first_row += rows
            total = total_ref[at, :]
            out[:, 0:width] = (grown[at, :] * (1.0 / total)).astype(out.dtype)
            spread = top_ref[at, :] + jnp.log(total)
            first = spread.astype(BF).astype(F32)
            second = (spread - first).astype(BF).astype(F32)
            third = spread - first - second
            lane = lax.broadcasted_iota(jnp.int32, (rows, LANES), 1)
            tail = jnp.where(lane == 0, first, jnp.where(lane == 1, second, jnp.where(lane == 2, third, 0.0)))
            out[:, width : width + LANES] = tail.astype(out.dtype)


def vocab_backward(first_ref, *refs):
    *pieces, spread_ref, id_ref, e_ref, so_far, out = refs
    total = so_far[...]
    index = lax.broadcasted_iota(jnp.int32, (out.shape[0], 1), 0) + first_ref[pl.program_id(0)]
    at = 0
    for piece in pieces:
        columns = slice(at, at + piece.shape[0])
        rows = piece[...]
        probs = jnp.exp(nt(e_ref[...], rows) - spread_ref[:, columns])
        hits = jnp.where(index == id_ref[:, columns], 1.0, 0.0)
        total = total + nn((LOSS_SCALE * (probs - hits)).astype(BF), rows)
        at += piece.shape[0]
    out[...] = total


def embed_backward(first_ref, *refs):
    *pieces, id_ref, so_far, out = refs
    total = jnp.zeros(out.shape, F32)
    index = lax.broadcasted_iota(jnp.int32, (out.shape[0], 1), 0) + first_ref[pl.program_id(0)]
    at = 0
    for piece in pieces:
        hits = jnp.where(index == id_ref[:, at : at + piece.shape[0]], 1.0, 0.0)
        total = total + nn(hits.astype(BF), piece[...])
        at += piece.shape[0]
    out[...] = so_far[...] + total * piece.shape[1] ** 0.5


def layer_forward(x, x_low, lens, me, weights):
    w_qkv, b_qkv, w_out, w_in, b_in, w_down, gains, shifts, gates = weights
    rows, width = x.shape
    tokens = 4 * rows
    outs = piece_outs(rows, width) + [sds((tokens, width), BF), sds((tokens, 3 * PART), BF), sds((tokens, PART), BF)]
    *parts, x_rel, proj, ctx_rel = kernel_call(
        attention_forward,
        "attention_forward",
        outs,
        [lens, me],
        gather_pieces(x_low) + [w_qkv, b_qkv, gates, w_out],
        [pltpu.VMEM((tokens, PART), BF)],
        flops=2 * tokens * width * 4 * PART,
    )
    near, far = reduce_pieces(*parts[1:])
    norm_outs = [sds((rows, width), F32), sds((rows, width), BF), sds((rows, width), F32), sds((rows, 1), F32)]
    hidden, hidden_low, normed_one, scale_one = kernel_call(
        norm_forward,
        "first_norm",
        norm_outs,
        [],
        [parts[0], near, far, x, shifts[0:1], gains[0:1], shifts[1:2]],
    )
    units = w_in.shape[1]
    outs = piece_outs(rows, width) + [sds((tokens, width), BF), sds((tokens, units), BF), sds((tokens, units), F32)]
    *parts, h_rel, act, slope = kernel_call(
        feed_forward,
        "feed_forward",
        outs,
        [],
        gather_pieces(hidden_low) + [w_in, b_in, w_down],
        flops=4 * tokens * width * units,
    )
    near, far = reduce_pieces(*parts[1:])
    out, out_low, normed_two, scale_two = kernel_call(
        norm_forward,
        "second_norm",
        norm_outs,
        [],
        [parts[0], near, far, hidden, shifts[2:3], gains[1:2], shifts[3:4]],
    )
    return out, out_low, (x_rel, proj, ctx_rel, h_rel, act, slope, normed_one, scale_one, normed_two, scale_two)


def layer_backward(d_two, pieces, lens, me, weights, saved, section, head_width, fill):
    w_qkv, b_qkv, w_out, w_in, b_in, w_down, gains, shifts, gates = weights
    x_rel, proj, ctx_rel, h_rel, act, slope, normed_one, scale_one = saved[:8]
    rows, width = d_two.shape
    tokens = 4 * rows
    units = w_in.shape[1]
    outs = piece_outs(rows, width) + [sds((tokens, width), BF), sds((tokens, units), BF), sds((1, units), F32)]
    *parts, d_rel, d_pre, d_b_in = kernel_call(
        feed_backward,
        "feed_backward",
        outs,
        [],
        pieces + [w_in, w_down, slope],
        flops=4 * tokens * width * units,
    )
    near, far = fill[0](reduce_pieces(*parts[1:]))
    d_w_down = tn(act, d_rel).astype(BF)
    d_w_in = tn(h_rel, d_pre).astype(BF)
    first = section == 0
    sent = swap(jnp.where(first, d_w_down, d_w_in), "section", 1)
    d_feed = plus(jnp.where(first, d_w_in, d_w_down), sent)
    outs = [sds((rows, width), F32), sds((rows, width), F32), sds((rows, width), BF), sds((8, width), F32)]
    _, d_one, d_one_low, sums = kernel_call(
        norm_backward,
        "first_norm_grad",
        outs,
        [],
        [parts[0], near, far, d_two, normed_one, scale_one, gains[0:1]],
    )
    pieces, d_feed = lax.optimization_barrier((gather_pieces(d_one_low), d_feed))
    pieces = fill[1](pieces)
    outs = piece_outs(rows, width) + [
        sds((tokens, width), BF),
        sds((tokens, 3 * PART), BF),
        sds((1, 3 * PART), F32),
        sds(gates.shape, F32),
    ]
    *parts, d_rel, dproj, d_b_qkv, d_gate = kernel_call(
        attention_backward,
        "attention_backward",
        outs,
        [lens, me],
        pieces + [w_qkv, gates, w_out, proj],
        [
            pltpu.VMEM((tokens, PART), BF),
            pltpu.VMEM((tokens, PART), F32),
            pltpu.VMEM((tokens, PART), F32),
            pltpu.VMEM((tokens, 3 * PART), BF),
        ],
        flops=2 * tokens * width * 4 * PART,
        vmem=40,
    )
    near, far = fill[2](reduce_pieces(*parts[1:]))
    d_w_qkv = tn(x_rel, dproj).astype(BF).reshape(width, 3, PART)[:, :, :head_width].reshape(width, 3 * head_width)
    d_w_out = tn(d_rel, ctx_rel).astype(BF)[:, :head_width]
    d_attn = halves(jnp.concatenate([d_w_qkv, d_w_out], axis=1), section)
    d_gate = (halves(d_gate.astype(BF).reshape(-1, d_gate.shape[2]), section))
    return (parts[0], near, far, d_one), (d_feed, d_attn, d_gate), (d_b_qkv, d_b_in, sums)


def head_blocks(pieces, embedding, outs):
    width = embedding.shape[1]
    vocab = embedding.shape[0]
    tokens = sum(p.shape[0] for p in pieces)
    wide = width + LANES
    return pl.pallas_call(
        functools.partial(head_forward, len(pieces)),
        name="head_forward",
        grid=(vocab // VOCAB_STEP,),
        in_specs=[pl.BlockSpec(p.shape, lambda i: (0, 0)) for p in pieces]
        + [pl.BlockSpec((VOCAB_STEP, width), lambda i: (i, 0))],
        out_specs=[pl.BlockSpec((rows, wide), lambda i: (0, 0)) for rows, _ in outs],
        out_shape=[sds((rows, wide), dtype) for rows, dtype in outs],
        scratch_shapes=[
            pltpu.VMEM((tokens, width), BF),
            pltpu.VMEM((tokens, width), F32),
            pltpu.VMEM((tokens, 1), F32),
            pltpu.VMEM((tokens, 1), F32),
        ],
        compiler_params=pltpu.CompilerParams(vmem_limit_bytes=44 * MIB),
        cost_estimate=pl.CostEstimate(
            flops=4 * tokens * vocab * width, bytes_accessed=2 * vocab * width, transcendentals=vocab * tokens
        ),
    )(*pieces, embedding)


def owned_rows(kernel, name, pieces, columns, firsts, so_far, rows=None):
    count, width = so_far.shape
    steps = firsts.shape[0]
    tokens = columns[0].shape[1]
    part = pl.BlockSpec((count // steps, width), lambda i: (i, 0))
    given = [] if rows is None else [rows]
    return pl.pallas_call(
        kernel,
        name=name,
        grid=(steps,),
        in_specs=scalar_specs(1)
        + [pl.BlockSpec(p.shape, lambda i: (0, 0)) for p in pieces]
        + [pl.BlockSpec((1, tokens), lambda i: (0, 0))] * len(columns)
        + [part] * (len(given) + 1),
        out_specs=part,
        out_shape=sds((count, width), F32),
        input_output_aliases={1 + len(pieces) + len(columns) + len(given): 0},
        compiler_params=pltpu.CompilerParams(vmem_limit_bytes=44 * MIB),
        cost_estimate=pl.CostEstimate(
            flops=0, bytes_accessed=0, transcendentals=0
        ),
    )(firsts, *pieces, *columns, *given, so_far)


def pad_parts(array, axis):
    pads = [(0, 0)] * array.ndim
    pads[axis] = (0, PART - array.shape[axis])
    return jnp.pad(array, pads)


def lookup_rows(ids, embedding):
    rows = embedding.shape[0]
    inside = (ids >= 0) & (ids < rows)
    found = jnp.where(inside[:, None], embedding[jnp.clip(ids, 0, rows - 1)], jnp.zeros((), BF))
    count = found.shape[0] // 4
    own, near, far, corner = [found[r * count : (r + 1) * count] for r in range(4)]
    near, far = reduce_pieces(near, far, corner[: count // 2], corner[count // 2 :])
    return own + near + far


def halves(array, section):
    half = array.shape[0] // 2
    mine = lax.dynamic_slice_in_dim(array, section * half, half, 0)
    other = lax.dynamic_slice_in_dim(array, (1 - section) * half, half, 0)
    return (mine.astype(F32) + swap(other, "section", 1).astype(F32)).astype(BF)


def dp_sum(arrays, turn):
    order = list(range(lax.axis_size("dp")))
    order = order[turn:] + order[:turn]
    return lax.psum(arrays, "dp", axis_index_groups=[order])


def plus(left, right):
    return (left.astype(F32) + right.astype(F32)).astype(BF)


def sum_over(array, axes):
    for axis in axes:
        bit = 1
        while bit < lax.axis_size(axis):
            array = array + swap(array, axis, bit)
            bit *= 2
    return array


def shards(
    token_ids,
    targets,
    lengths,
    embedding,
    w_qkv,
    b_qv,
    w_out,
    w_in,
    b_in,
    w_down,
    norm_gains,
    shifts,
    mask_logits,
    mask_noise,
):
    section = lax.axis_index("section")
    first = section == 0
    place = lax.axis_index("tensor")
    me = place[None].astype(jnp.int32)
    tokens = token_ids.shape[1]
    rows = tokens // lax.axis_size("tensor")
    width = embedding.shape[1]
    vocab_rows = embedding.shape[0]
    vocab_start = place * vocab_rows
    head_width = w_qkv.shape[3]
    order = place ^ jnp.arange(4, dtype=jnp.int32)

    gate_own = jax.nn.sigmoid(mask_logits[0] + mask_noise[0])
    small = jnp.concatenate(
        [
            norm_gains[0],
            shifts[0],
            b_in[0][None],
            jnp.pad(b_qv[0], ((0, 0), (0, width - head_width))),
        ]
    )
    held = (w_qkv[0].reshape(width, 3 * head_width), w_out[0], w_in[0], w_down[0], small, gate_own)
    brought = jax.tree.map(lambda a: swap(a, "section", 1), held)

    def weights_of(layer):
        kept = section == layer
        wq, wo, wi, wd, vec, gates = jax.tree.map(lambda a, b: jnp.where(kept, a, b), held, brought)
        bias = jnp.concatenate(
            [
                vec[7:8, :PART],
                jnp.zeros((1, PART), F32),
                vec[8:9, :PART],
            ],
            axis=1,
        )
        wq = pad_parts(wq.reshape(width, 3, head_width), 2).reshape(width, 3 * PART)
        return (wq, bias, pad_parts(wo, 0), wi, vec[6:7], wd, vec[0:2], vec[2:6], gates)

    layers = [weights_of(0), weights_of(1)]
    lens = lax.dynamic_index_in_dim(lengths, section, 0, keepdims=False)

    def mine(ids):
        row = lax.dynamic_index_in_dim(ids, section, 0, keepdims=False)
        return row.reshape(4, rows)[order].reshape(tokens) - vocab_start

    target_local, token_local = mine(targets), mine(token_ids)
    x = lookup_rows(token_local, embedding).astype(F32) * width**0.5
    target_rows = lookup_rows(target_local, embedding)
    hidden, hidden_low, saved_first = layer_forward(x, x.astype(BF), lens, me, layers[0])
    final, final_low, saved_last = layer_forward(hidden, hidden_low, lens, me, layers[1])

    dp = lax.axis_size("dp")
    pieces = gather_pieces(final_low)
    rows_of = [final_low] + [swap(final_low, "dp", other) for other in range(1, dp)]
    (own,) = head_blocks(pieces[:1], embedding, [(rows, F32)])
    own, *pieces[1:] = lax.optimization_barrier((own, *pieces[1:]))
    near, far, corner = head_blocks(pieces[1:], embedding, [(rows, BF)] * 3)
    there = [pieces] + [gather_pieces(r) for r in rows_of[1:]]
    near, far, corner, there[1:2] = lax.optimization_barrier((near, far, corner, there[1:2]))
    near, far, corner = swap(near, "tensor", 1), swap(far, "tensor", 2), swap(corner, "tensor", 3)
    outs = [sds((rows, width), F32), sds((rows, width), BF), sds((8, width), F32), sds((8, rows), F32)]
    d_two, d_two_low, sums_two_last, spread = kernel_call(
        merge_head,
        "merge_head",
        outs,
        [],
        [own, near, far, corner, target_rows, saved_last[8], saved_last[9], layers[1][6][1:2]],
    )
    d_pieces = gather_pieces(d_two_low)

    half_vocab = vocab_rows // 2
    share = half_vocab // dp
    steps = 2 if (share // 2) % 16 == 0 else 1
    starts = [lax.axis_index("dp") * share + c * half_vocab for c in (section, 1 - section)]
    firsts = [(start + jnp.arange(0, share, share // steps, dtype=jnp.int32)).astype(jnp.int32) for start in starts]
    my_rows = [lax.dynamic_slice_in_dim(embedding, start, share, 0) for start in starts]
    spread = jnp.concatenate([spread[0:1]] + [swap(spread, "tensor", bit)[0:1] for bit in (1, 2, 3)], axis=1)
    d_rows = [jnp.zeros((share, width), F32)] * 2
    id_pair = jnp.stack([token_local, target_local])
    id_pairs = [id_pair] + [swap(id_pair, "dp", other) for other in range(1, dp)]
    spreads = [spread] + [swap(spread, "dp", other) for other in range(1, dp)]

    def dense_half(values, half):
        total = d_rows[half]
        for others in groups(4):
            found = sum([there[other] for other in others], [])
            columns = [jnp.concatenate([spreads[other] for other in others], axis=1)]
            columns += [jnp.concatenate([id_pairs[other][1:2] for other in others], axis=1)]
            total = owned_rows(vocab_backward, "vocab_backward", found, columns, firsts[half], total, my_rows[half])
        values, d_rows[half] = lax.optimization_barrier((values, total))
        return values

    def groups(size):
        return [range(at, min(at + size, dp)) for at in range(0, dp, size)]

    sums = []

    def early_sum(d_feed, turn):
        sums.append(dp_sum(d_feed, turn))

    def held(values, k):
        values, sums[k] = lax.optimization_barrier((values, sums[k]))
        return values

    d_x, d_rest_last, vecs_last = layer_backward(
        d_two,
        d_pieces,
        lens,
        me,
        layers[1],
        saved_last,
        section,
        head_width,
        [lambda v: v] * 3,
    )
    outs = [sds((rows, width), F32), sds((rows, width), F32), sds((rows, width), BF), sds((8, width), F32)]
    grad_last, d_two, d_two_low, sums_two_first = kernel_call(
        norm_backward,
        "second_norm_grad",
        outs,
        [],
        list(d_x) + [saved_first[8], saved_first[9], layers[0][6][1:2]],
    )
    d_pieces, d_rest_last, there[1:] = lax.optimization_barrier((gather_pieces(d_two_low), d_rest_last, there[1:]))
    early_sum(d_rest_last, 0)
    d_x, d_rest_first, vecs_first = layer_backward(
        d_two,
        d_pieces,
        lens,
        me,
        layers[0],
        saved_first,
        section,
        head_width,
        [lambda v: v, lambda v: v, lambda v: held(dense_half(v, 1), 0)],
    )
    def vec_rows(vecs, sums_two):
        d_b_qkv, d_b_in, sums_one = vecs
        wide = jnp.concatenate([sums_one[0:1], sums_two[0:1], sums_one[2:3], sums_one[1:2], sums_two[2:3], sums_two[1:2]])
        narrow = jnp.concatenate(
            [jnp.pad(d_b_qkv[:, :PART], ((0, 0), (0, width - PART))), jnp.pad(d_b_qkv[:, 2 * PART :], ((0, 0), (0, width - PART))), d_b_in]
        )
        spread_out = jnp.where((jnp.arange(4) == place)[:, None, None], narrow[None], 0.0).reshape(12, width)
        return jnp.concatenate([wide, spread_out])

    vecs = jnp.stack([vec_rows(vecs_first, sums_two_first), vec_rows(vecs_last, sums_two_last)])
    vecs = sum_over(vecs, ("tensor", "section")).astype(BF).reshape(-1, width)
    d_feed_first, d_attn, d_gate = d_rest_first
    d_x, d_feed_first, d_attn, d_gate, vecs = lax.optimization_barrier((d_x, d_feed_first, d_attn, d_gate, vecs))
    early_sum((d_feed_first, jnp.concatenate([d_attn, vecs]), d_gate), 1)
    grad_first = d_x[3] + (d_x[0] + d_x[1].astype(F32) + d_x[2].astype(F32))

    rows_here = grad_first.astype(BF)
    arriving = [swap(rows_here, "dp", other) for other in range(1, dp)]
    own_pieces, arriving = dense_half((gather_pieces(rows_here), arriving), 0)
    found = [own_pieces] + [gather_pieces(r) for r in arriving]
    for others in groups(3):
        ids = jnp.concatenate([id_pairs[other][0:1] for other in others], axis=1)
        pieces = sum([found[other] for other in others], [])
        d_rows = [
            owned_rows(embed_backward, "embed_backward", pieces, [ids], *part)
            for part in reversed(list(zip(firsts, d_rows)))
        ][::-1]
    d_embedding = d_rows[0] + swap(d_rows[1].astype(BF), "section", 1).astype(F32)

    def assembled(low_layer, high_layer):
        got = swap(jnp.where(first, high_layer, low_layer), "section", 1)
        return jnp.where(first, low_layer, got).astype(F32), jnp.where(first, got, high_layer).astype(F32)

    grads_last, (d_feed, d_attn, d_gate) = sums
    grads_first = (d_feed, d_attn[: width // 2], d_gate)
    vecs = d_attn[width // 2 :].reshape(2, -1, width)
    vecs = lax.dynamic_index_in_dim(vecs, section, 0, keepdims=False).astype(F32)
    narrow = lax.dynamic_slice_in_dim(vecs, 6 + 3 * place, 3, 0)
    (g_in, g_down), attn, gate = jax.tree.map(assembled, grads_first, grads_last)
    attn = jnp.concatenate(attn)
    g_qkv = attn[:, : 3 * head_width].reshape(width, 3, head_width)
    g_out = attn[:, 3 * head_width :].T
    g_mask = jnp.concatenate(gate).reshape(gate_own.shape) * gate_own * (1.0 - gate_own)

    def placed_rows(low_layer, high_layer):
        got = swap(jnp.where(first, high_layer, low_layer), "section", 1)
        return jnp.where(first, jnp.stack([low_layer, got]), jnp.stack([got, high_layer]))

    return (
        placed_rows(hidden, final)[None],
        placed_rows(grad_first, grad_last)[None],
        d_embedding,
        g_qkv[None],
        narrow[None, 0:2, :head_width],
        g_out[None],
        g_in[None],
        narrow[None, 2],
        g_down[None],
        vecs[None, 0:2],
        vecs[None, 2:6],
        g_mask[None],
    )


def solution(mesh):
    placed = (
        P("dp", None),
        P("dp", None),
        P("dp", None),
        P("tensor", None),
        P("section", None, None, "tensor"),
        P("section", None, "tensor"),
        P("section", "tensor", None),
        P("section", None, "tensor"),
        P("section", "tensor"),
        P("section", "tensor", None),
        P("section", None, None),
        P("section", None, None),
        P("section", "tensor", None, None),
        P("section", "tensor", None, None),
    )
    return jax.shard_map(
        shards,
        mesh=mesh,
        in_specs=placed,
        out_specs=(
            P("section", "dp", "tensor", None),
            P("section", "dp", "tensor", None),
            P(("tensor", "section", "dp"), None),
            P("section", None, None, "tensor"),
            P("section", None, "tensor"),
            P("section", "tensor", None),
            P("section", None, "tensor"),
            P("section", "tensor"),
            P("section", "tensor", None),
            P("section", None, None),
            P("section", None, None),
            P("section", "tensor", None, None),
        ),
        check_vma=False,
    )
```

```python
import functools

import jax
import jax.numpy as jnp
from jax import lax
from jax.experimental import pallas as pl
from jax.experimental.pallas import tpu as pltpu
from jax.sharding import PartitionSpec as P

BUCKET = 128
MAXLEN = 512
EPSILON = 1e-12
LOSS_SCALE = 16.0
BF = jnp.bfloat16
F32 = jnp.float32
MIB = 1 << 20
LANES = 128
HEAD_DIM = 64
VOCAB_STEP = 1536
HEAD_CHUNK = 256


def nn(left, right):
    return jnp.dot(left, right, preferred_element_type=F32)


def nt(left, right):
    return lax.dot_general(left, right, (((1,), (1,)), ((), ())), preferred_element_type=F32)


def tn(left, right):
    return lax.dot_general(left, right, (((0,), (0,)), ((), ())), preferred_element_type=F32)


def sds(shape, dtype):
    return jax.ShapeDtypeStruct(shape, dtype)


def whole_specs(count):
    return [pl.BlockSpec(memory_space=pltpu.VMEM)] * count


def scalar_specs(count):
    return [pl.BlockSpec(memory_space=pltpu.SMEM)] * count


def kernel_call(kernel, name, outs, scalars, arrays, scratch=(), flops=0, vmem=32):
    moved = sum(a.size * a.dtype.itemsize for a in arrays)
    moved += sum(jnp.dtype(o.dtype).itemsize * functools.reduce(lambda a, b: a * b, o.shape, 1) for o in outs)
    return pl.pallas_call(
        kernel,
        name=name,
        out_shape=outs,
        in_specs=scalar_specs(len(scalars)) + whole_specs(len(arrays)),
        out_specs=whole_specs(len(outs)),
        scratch_shapes=list(scratch),
        compiler_params=pltpu.CompilerParams(vmem_limit_bytes=vmem * MIB),
        cost_estimate=pl.CostEstimate(flops=0, bytes_accessed=0, transcendentals=0),
    )(*scalars, *arrays)


def swap(array, axis, bit):
    count = lax.axis_size(axis)
    return lax.ppermute(array, axis, [(i, i ^ bit) for i in range(count)])


def gather_pieces(own):
    half = own.shape[0] // 2
    near = swap(own, "tensor", 1)
    far = swap(own, "tensor", 2)
    corner_low = swap(near[:half], "tensor", 2)
    corner_high = swap(far[half:], "tensor", 1)
    return [own, near, far, corner_low, corner_high]


def reduce_pieces(near, far, corner_low, corner_high):
    half = near.shape[0] // 2
    low = swap(corner_low, "tensor", 1)
    high = swap(corner_high, "tensor", 2)
    far_sum = jnp.concatenate([(far[:half].astype(F32) + low.astype(F32)).astype(BF), far[half:]])
    near_sum = jnp.concatenate([near[:half], (near[half:].astype(F32) + high.astype(F32)).astype(BF)])
    return swap(near_sum, "tensor", 1), swap(far_sum, "tensor", 2)


def copy_pieces(pieces, target):
    at = 0
    for piece in pieces:
        rows = piece.shape[0]
        target[at : at + rows, :] = piece[...]
        at += rows


def store_block(r, value, own, near, far, corner_low, corner_high):
    half = near.shape[0] // 2
    if r == 0:
        own[...] = value
    elif r == 1:
        near[...] = value.astype(BF)
    elif r == 2:
        far[...] = value.astype(BF)
    else:
        corner_low[...] = value[:half].astype(BF)
        corner_high[...] = value[half:].astype(BF)


def piece_outs(rows, width):
    return [
        sds((rows, width), F32),
        sds((rows, width), BF),
        sds((rows, width), BF),
        sds((rows // 2, width), BF),
        sds((rows // 2, width), BF),
    ]


def sequence_of(bucket, len_ref):
    start, length, total = jnp.int32(0), len_ref[0], jnp.int32(0)
    for i in range(len_ref.shape[0]):
        begun = bucket >= total
        start = jnp.where(begun, total, start)
        length = jnp.where(begun, len_ref[i], length)
        total = total + len_ref[i]
    return start, length


def half_masks():
    lane = lax.broadcasted_iota(jnp.int32, (1, LANES), 1)
    low = (lane < HEAD_DIM).astype(F32)
    return [low.astype(BF), (1.0 - low).astype(BF)], lane < HEAD_DIM


TILES = ((0, (0, 1)), (1, (2,)))
PART = 2 * LANES


def block_rows(me, r, rows):
    return pl.ds(pl.multiple_of((me ^ r) * rows, rows), rows)


def attention_forward(len_ref, me_ref, *refs):
    pieces, refs = refs[:5], refs[5:]
    w_ref, b_ref, g_ref, wo_ref, own, near, far, c_low, c_high, x_rel, proj, ctx_rel, ctx = refs
    me = me_ref[0]
    rows = own.shape[0]
    tokens = proj.shape[0]
    copy_pieces(pieces, x_rel)

    @pl.loop(0, 4)
    def project(r):
        value = nn(x_rel[pl.ds(pl.multiple_of(r * rows, rows), rows), :], w_ref[...]) + b_ref[...]
        proj[block_rows(me, r, rows), :] = value.astype(BF)

    masks, low_lane = half_masks()

    @pl.loop(0, tokens // BUCKET)
    def attend(bucket):
        start, length = sequence_of(bucket, len_ref)
        q_rows = pl.ds(pl.multiple_of(bucket * BUCKET, BUCKET), BUCKET)
        gate_rows = pl.ds(pl.multiple_of((bucket - start) * BUCKET, BUCKET), BUCKET)

        def body(size):
            k_rows = pl.ds(pl.multiple_of(start * BUCKET, BUCKET), size)
            for tile, heads in TILES:
                at = tile * LANES
                q = proj[q_rows, at : at + LANES]
                k = proj[k_rows, PART + at : PART + at + LANES]
                v = proj[k_rows, 2 * PART + at : 2 * PART + at + LANES]
                mixed = []
                for i, head in enumerate(heads):
                    qm = q * masks[i] if len(heads) > 1 else q
                    scores = nt(qm, k) * HEAD_DIM ** (-0.5)
                    powers = jnp.exp(scores - jnp.max(scores, axis=-1, keepdims=True))
                    attention = powers * (1.0 / jnp.sum(powers, axis=-1, keepdims=True))
                    gated = (attention * g_ref[head, gate_rows, 0:size]).astype(BF)
                    mixed.append(nn(gated, v))
                value = jnp.where(low_lane, mixed[0], mixed[1]) if len(heads) > 1 else mixed[0]
                ctx[q_rows, at : at + LANES] = value.astype(BF)

        for buckets in range(1, MAXLEN // BUCKET + 1):
            pl.when(length == buckets)(functools.partial(body, buckets * BUCKET))

    for r in range(4):
        block = ctx[block_rows(me, r, rows), :]
        ctx_rel[r * rows : (r + 1) * rows, :] = block
        store_block(r, nn(block, wo_ref[...]), own, near, far, c_low, c_high)


def attention_backward(len_ref, me_ref, *refs):
    pieces, refs = refs[:5], refs[5:]
    w_ref, g_ref, wo_ref, proj, own, near, far, c_low, c_high, d_rel, dproj_rel, d_bias, d_gate, d_ctx, d_key, d_val, dproj = refs
    me = me_ref[0]
    rows = own.shape[0]
    tokens = proj.shape[0]
    copy_pieces(pieces, d_rel)

    @pl.loop(0, 4)
    def context_grad(r):
        value = nt(d_rel[pl.ds(pl.multiple_of(r * rows, rows), rows), :], wo_ref[...])
        d_ctx[block_rows(me, r, rows), :] = value.astype(BF)

    d_gate[...] = jnp.zeros_like(d_gate)
    d_key[...] = jnp.zeros_like(d_key)
    d_val[...] = jnp.zeros_like(d_val)
    masks, low_lane = half_masks()

    @pl.loop(0, tokens // BUCKET)
    def attend(bucket):
        start, length = sequence_of(bucket, len_ref)
        q_rows = pl.ds(pl.multiple_of(bucket * BUCKET, BUCKET), BUCKET)
        gate_rows = pl.ds(pl.multiple_of((bucket - start) * BUCKET, BUCKET), BUCKET)

        def body(size):
            k_rows = pl.ds(pl.multiple_of(start * BUCKET, BUCKET), size)
            for tile, heads in TILES:
                at = tile * LANES
                q = proj[q_rows, at : at + LANES]
                k = proj[k_rows, PART + at : PART + at + LANES]
                v = proj[k_rows, 2 * PART + at : 2 * PART + at + LANES]
                d_out = d_ctx[q_rows, at : at + LANES]
                d_q = []
                key_sum = val_sum = None
                for i, head in enumerate(heads):
                    qm = q * masks[i] if len(heads) > 1 else q
                    dm = d_out * masks[i] if len(heads) > 1 else d_out
                    scores = nt(qm, k) * HEAD_DIM ** (-0.5)
                    powers = jnp.exp(scores - jnp.max(scores, axis=-1, keepdims=True))
                    attention = powers * (1.0 / jnp.sum(powers, axis=-1, keepdims=True))
                    gate = g_ref[head, gate_rows, 0:size]
                    d_mixed = nt(dm, v)
                    d_gate[head, gate_rows, 0:size] += d_mixed * attention
                    d_prob = d_mixed * gate
                    inner = jnp.sum(d_prob * attention, axis=-1, keepdims=True)
                    d_scores = (attention * (d_prob - inner)).astype(BF)
                    gated = (attention * gate).astype(BF)
                    val = tn(gated, dm)
                    key = tn(d_scores, qm)
                    val_sum = val if val_sum is None else val_sum + val
                    key_sum = key if key_sum is None else key_sum + key
                    d_q.append(nn(d_scores, k))
                value = jnp.where(low_lane, d_q[0], d_q[1]) if len(heads) > 1 else d_q[0]
                dproj[q_rows, at : at + LANES] = (value * HEAD_DIM ** (-0.5)).astype(BF)
                d_key[k_rows, at : at + LANES] += key_sum
                d_val[k_rows, at : at + LANES] += val_sum

        for buckets in range(1, MAXLEN // BUCKET + 1):
            pl.when(length == buckets)(functools.partial(body, buckets * BUCKET))

    dproj[:, PART : 2 * PART] = (d_key[...] * HEAD_DIM ** (-0.5)).astype(BF)
    dproj[:, 2 * PART : 3 * PART] = d_val[...].astype(BF)
    sums = jnp.zeros((1, dproj.shape[1]), F32)
    for r in range(4):
        block = dproj[block_rows(me, r, rows), :]
        dproj_rel[r * rows : (r + 1) * rows, :] = block
        sums = sums + jnp.sum(block.astype(F32), axis=0, keepdims=True)
        store_block(r, nt(block, w_ref[...]), own, near, far, c_low, c_high)
    d_bias[...] = sums


def feed_forward(*refs):
    pieces, refs = refs[:5], refs[5:]
    w_in, b_in, w_down, own, near, far, c_low, c_high, h_rel, act, slope = refs
    rows = own.shape[0]
    copy_pieces(pieces, h_rel)
    for r in range(4):
        at = slice(r * rows, (r + 1) * rows)
        pre = nn(h_rel[at, :], w_in[...]) + b_in[...]
        below = 0.5 * (1.0 + lax.erf(pre * 0.7071067811865476))
        active = (pre * below).astype(BF)
        act[at, :] = active
        slope[at, :] = below + pre * jnp.exp(-0.5 * pre * pre) * 0.3989422804014327
        store_block(r, nn(active, w_down[...]), own, near, far, c_low, c_high)


def feed_backward(*refs):
    pieces, refs = refs[:5], refs[5:]
    w_in, w_down, slope, own, near, far, c_low, c_high, d_rel, d_pre, d_bias = refs
    rows = own.shape[0]
    copy_pieces(pieces, d_rel)
    sums = jnp.zeros((1, d_pre.shape[1]), F32)
    for r in range(4):
        at = slice(r * rows, (r + 1) * rows)
        value = (slope[at, :] * nt(d_rel[at, :], w_down[...])).astype(BF)
        d_pre[at, :] = value
        sums = sums + jnp.sum(value.astype(F32), axis=0, keepdims=True)
        store_block(r, nt(value, w_in[...]), own, near, far, c_low, c_high)
    d_bias[...] = sums


def norm_forward(own, near, far, residual, bias, gain, shift, hidden, hidden_low, normed_ref, scale_ref):
    value = residual[...] + (own[...] + near[...].astype(F32) + far[...].astype(F32)) + bias[...]
    centered = value - jnp.mean(value, axis=-1, keepdims=True)
    scale = lax.rsqrt(jnp.mean(centered * centered, axis=-1, keepdims=True) + EPSILON)
    normed = centered * scale
    out = normed * gain[...] + shift[...]
    hidden[...] = out
    hidden_low[...] = out.astype(BF)
    normed_ref[...] = normed
    scale_ref[...] = scale


def norm_grad(grad, normed, scale, gain, d_sum_ref, d_low_ref, sums_ref):
    scaled = grad * gain
    d_sum = scale * (
        scaled
        - jnp.mean(scaled, axis=-1, keepdims=True)
        - normed * jnp.mean(scaled * normed, axis=-1, keepdims=True)
    )
    d_sum_ref[...] = d_sum
    d_low_ref[...] = d_sum.astype(BF)
    sums_ref[0:1, :] = jnp.sum(grad * normed, axis=0, keepdims=True)
    sums_ref[1:2, :] = jnp.sum(grad, axis=0, keepdims=True)
    sums_ref[2:3, :] = jnp.sum(d_sum, axis=0, keepdims=True)


def norm_backward(own, near, far, residual, normed, scale, gain, d_out, d_sum, d_low, sums):
    grad = residual[...] + (own[...] + near[...].astype(F32) + far[...].astype(F32))
    d_out[...] = grad
    norm_grad(grad, normed[...], scale[...], gain[...], d_sum, d_low, sums)


def merge_head(own, near, far, corner, target_rows, normed, scale, gain, d_sum, d_low, sums, spread_ref):
    width = target_rows.shape[1]
    blocks = [own[...], near[...].astype(F32), far[...].astype(F32), corner[...].astype(F32)]
    spreads = [jnp.sum(block[:, width : width + 3], axis=-1, keepdims=True) for block in blocks]
    top = functools.reduce(jnp.maximum, spreads)
    shares = [jnp.exp(spread - top) for spread in spreads]
    total = functools.reduce(lambda a, b: a + b, shares)
    expected = functools.reduce(
        lambda a, b: a + b, [block[:, :width] * (share / total) for block, share in zip(blocks, shares)]
    )
    grad = LOSS_SCALE * (expected - target_rows[...].astype(F32))
    norm_grad(grad, normed[...], scale[...], gain[...], d_sum, d_low, sums)
    spread = top + jnp.log(total)
    spread_ref[...] = jnp.transpose(jnp.broadcast_to(spread, (spread.shape[0], LANES)))[0:8, :]


def head_forward(count, *refs):
    pieces, refs = refs[:count], refs[count:]
    e_ref, *outs = refs[:-4]
    x_rel, grown, top_ref, total_ref = refs[-4:]
    step = pl.program_id(0)
    tokens, width = x_rel.shape
    chunks = [slice(at, at + HEAD_CHUNK) for at in range(0, tokens, HEAD_CHUNK)]

    @pl.when(step == 0)
    def begin():
        copy_pieces(pieces, x_rel)
        grown[...] = jnp.zeros_like(grown)
        top_ref[...] = jnp.full_like(top_ref, -1e30)
        total_ref[...] = jnp.zeros_like(total_ref)

    logits = [nt(x_rel[at, :], e_ref[...]) for at in chunks]
    shares = []
    for at, block in zip(chunks, logits):
        old = top_ref[at, :]
        top = jnp.maximum(old, jnp.max(block, axis=1, keepdims=True))
        fade = jnp.exp(old - top)
        powers = jnp.exp(block - top)
        total_ref[at, :] = total_ref[at, :] * fade + jnp.sum(powers, axis=1, keepdims=True)
        top_ref[at, :] = top
        shares.append((fade, powers.astype(BF)))
    for at, (fade, powers) in zip(chunks, shares):
        grown[at, :] = grown[at, :] * fade + nn(powers, e_ref[...])

    @pl.when(step == pl.num_programs(0) - 1)
    def end():
        first_row = 0
        for out in outs:
            rows = out.shape[0]
            at = slice(first_row, first_row + rows)
            first_row += rows
            total = total_ref[at, :]
            out[:, 0:width] = (grown[at, :] * (1.0 / total)).astype(out.dtype)
            spread = top_ref[at, :] + jnp.log(total)
            first = spread.astype(BF).astype(F32)
            second = (spread - first).astype(BF).astype(F32)
            third = spread - first - second
            lane = lax.broadcasted_iota(jnp.int32, (rows, LANES), 1)
            tail = jnp.where(lane == 0, first, jnp.where(lane == 1, second, jnp.where(lane == 2, third, 0.0)))
            out[:, width : width + LANES] = tail.astype(out.dtype)


def vocab_backward(first_ref, *refs):
    *pieces, spread_ref, id_ref, e_ref, so_far, out = refs
    total = so_far[...]
    index = lax.broadcasted_iota(jnp.int32, (out.shape[0], 1), 0) + first_ref[pl.program_id(0)]
    at = 0
    for piece in pieces:
        columns = slice(at, at + piece.shape[0])
        rows = piece[...]
        probs = jnp.exp(nt(e_ref[...], rows) - spread_ref[:, columns])
        hits = jnp.where(index == id_ref[:, columns], 1.0, 0.0)
        total = total + nn((LOSS_SCALE * (probs - hits)).astype(BF), rows)
        at += piece.shape[0]
    out[...] = total


def embed_backward(first_ref, *refs):
    *pieces, id_ref, so_far, out = refs
    total = jnp.zeros(out.shape, F32)
    index = lax.broadcasted_iota(jnp.int32, (out.shape[0], 1), 0) + first_ref[pl.program_id(0)]
    at = 0
    for piece in pieces:
        hits = jnp.where(index == id_ref[:, at : at + piece.shape[0]], 1.0, 0.0)
        total = total + nn(hits.astype(BF), piece[...])
        at += piece.shape[0]
    out[...] = so_far[...] + total * piece.shape[1] ** 0.5


def layer_forward(x, x_low, lens, me, weights):
    w_qkv, b_qkv, w_out, w_in, b_in, w_down, gains, shifts, gates = weights
    rows, width = x.shape
    tokens = 4 * rows
    outs = piece_outs(rows, width) + [sds((tokens, width), BF), sds((tokens, 3 * PART), BF), sds((tokens, PART), BF)]
    *parts, x_rel, proj, ctx_rel = kernel_call(
        attention_forward,
        "attention_forward",
        outs,
        [lens, me],
        gather_pieces(x_low) + [w_qkv, b_qkv, gates, w_out],
        [pltpu.VMEM((tokens, PART), BF)],
        flops=2 * tokens * width * 4 * PART,
    )
    near, far = reduce_pieces(*parts[1:])
    norm_outs = [sds((rows, width), F32), sds((rows, width), BF), sds((rows, width), F32), sds((rows, 1), F32)]
    hidden, hidden_low, normed_one, scale_one = kernel_call(
        norm_forward,
        "first_norm",
        norm_outs,
        [],
        [parts[0], near, far, x, shifts[0:1], gains[0:1], shifts[1:2]],
    )
    units = w_in.shape[1]
    outs = piece_outs(rows, width) + [sds((tokens, width), BF), sds((tokens, units), BF), sds((tokens, units), F32)]
    *parts, h_rel, act, slope = kernel_call(
        feed_forward,
        "feed_forward",
        outs,
        [],
        gather_pieces(hidden_low) + [w_in, b_in, w_down],
        flops=4 * tokens * width * units,
    )
    near, far = reduce_pieces(*parts[1:])
    out, out_low, normed_two, scale_two = kernel_call(
        norm_forward,
        "second_norm",
        norm_outs,
        [],
        [parts[0], near, far, hidden, shifts[2:3], gains[1:2], shifts[3:4]],
    )
    return out, out_low, (x_rel, proj, ctx_rel, h_rel, act, slope, normed_one, scale_one, normed_two, scale_two)


def layer_backward(d_two, pieces, lens, me, weights, saved, section, head_width, fill):
    w_qkv, b_qkv, w_out, w_in, b_in, w_down, gains, shifts, gates = weights
    x_rel, proj, ctx_rel, h_rel, act, slope, normed_one, scale_one = saved[:8]
    rows, width = d_two.shape
    tokens = 4 * rows
    units = w_in.shape[1]
    outs = piece_outs(rows, width) + [sds((tokens, width), BF), sds((tokens, units), BF), sds((1, units), F32)]
    *parts, d_rel, d_pre, d_b_in = kernel_call(
        feed_backward,
        "feed_backward",
        outs,
        [],
        pieces + [w_in, w_down, slope],
        flops=4 * tokens * width * units,
    )
    near, far = fill[0](reduce_pieces(*parts[1:]))
    d_w_down = tn(act, d_rel).astype(BF)
    d_w_in = tn(h_rel, d_pre).astype(BF)
    first = section == 0
    sent = swap(jnp.where(first, d_w_down, d_w_in), "section", 1)
    d_feed = plus(jnp.where(first, d_w_in, d_w_down), sent)
    outs = [sds((rows, width), F32), sds((rows, width), F32), sds((rows, width), BF), sds((8, width), F32)]
    _, d_one, d_one_low, sums = kernel_call(
        norm_backward,
        "first_norm_grad",
        outs,
        [],
        [parts[0], near, far, d_two, normed_one, scale_one, gains[0:1]],
    )
    pieces, d_feed = lax.optimization_barrier((gather_pieces(d_one_low), d_feed))
    pieces = fill[1](pieces)
    outs = piece_outs(rows, width) + [
        sds((tokens, width), BF),
        sds((tokens, 3 * PART), BF),
        sds((1, 3 * PART), F32),
        sds(gates.shape, F32),
    ]
    *parts, d_rel, dproj, d_b_qkv, d_gate = kernel_call(
        attention_backward,
        "attention_backward",
        outs,
        [lens, me],
        pieces + [w_qkv, gates, w_out, proj],
        [
            pltpu.VMEM((tokens, PART), BF),
            pltpu.VMEM((tokens, PART), F32),
            pltpu.VMEM((tokens, PART), F32),
            pltpu.VMEM((tokens, 3 * PART), BF),
        ],
        flops=2 * tokens * width * 4 * PART,
        vmem=40,
    )
    near, far = fill[2](reduce_pieces(*parts[1:]))
    d_w_qkv = tn(x_rel, dproj).astype(BF).reshape(width, 3, PART)[:, :, :head_width].reshape(width, 3 * head_width)
    d_w_out = tn(d_rel, ctx_rel).astype(BF)[:, :head_width]
    d_attn = halves(jnp.concatenate([d_w_qkv, d_w_out], axis=1), section)
    d_gate = (halves(d_gate.astype(BF).reshape(-1, d_gate.shape[2]), section))
    return (parts[0], near, far, d_one), (d_feed, d_attn, d_gate), (d_b_qkv, d_b_in, sums)


def head_blocks(pieces, embedding, outs):
    width = embedding.shape[1]
    vocab = embedding.shape[0]
    tokens = sum(p.shape[0] for p in pieces)
    wide = width + LANES
    return pl.pallas_call(
        functools.partial(head_forward, len(pieces)),
        name="head_forward",
        grid=(vocab // VOCAB_STEP,),
        in_specs=[pl.BlockSpec(p.shape, lambda i: (0, 0)) for p in pieces]
        + [pl.BlockSpec((VOCAB_STEP, width), lambda i: (i, 0))],
        out_specs=[pl.BlockSpec((rows, wide), lambda i: (0, 0)) for rows, _ in outs],
        out_shape=[sds((rows, wide), dtype) for rows, dtype in outs],
        scratch_shapes=[
            pltpu.VMEM((tokens, width), BF),
            pltpu.VMEM((tokens, width), F32),
            pltpu.VMEM((tokens, 1), F32),
            pltpu.VMEM((tokens, 1), F32),
        ],
        compiler_params=pltpu.CompilerParams(vmem_limit_bytes=44 * MIB),
        cost_estimate=pl.CostEstimate(flops=0, bytes_accessed=0, transcendentals=0),
    )(*pieces, embedding)


def owned_rows(kernel, name, pieces, columns, firsts, so_far, rows=None):
    count, width = so_far.shape
    steps = firsts.shape[0]
    tokens = columns[0].shape[1]
    part = pl.BlockSpec((count // steps, width), lambda i: (i, 0))
    given = [] if rows is None else [rows]
    return pl.pallas_call(
        kernel,
        name=name,
        grid=(steps,),
        in_specs=scalar_specs(1)
        + [pl.BlockSpec(p.shape, lambda i: (0, 0)) for p in pieces]
        + [pl.BlockSpec((1, tokens), lambda i: (0, 0))] * len(columns)
        + [part] * (len(given) + 1),
        out_specs=part,
        out_shape=sds((count, width), F32),
        input_output_aliases={1 + len(pieces) + len(columns) + len(given): 0},
        compiler_params=pltpu.CompilerParams(vmem_limit_bytes=44 * MIB),
        cost_estimate=pl.CostEstimate(flops=0, bytes_accessed=0, transcendentals=0),
    )(firsts, *pieces, *columns, *given, so_far)


def pad_parts(array, axis):
    pads = [(0, 0)] * array.ndim
    pads[axis] = (0, PART - array.shape[axis])
    return jnp.pad(array, pads)


def lookup_rows(ids, embedding):
    rows = embedding.shape[0]
    inside = (ids >= 0) & (ids < rows)
    found = jnp.where(inside[:, None], embedding[jnp.clip(ids, 0, rows - 1)], jnp.zeros((), BF))
    count = found.shape[0] // 4
    own, near, far, corner = [found[r * count : (r + 1) * count] for r in range(4)]
    near, far = reduce_pieces(near, far, corner[: count // 2], corner[count // 2 :])
    return own + near + far


def halves(array, section):
    half = array.shape[0] // 2
    mine = lax.dynamic_slice_in_dim(array, section * half, half, 0)
    other = lax.dynamic_slice_in_dim(array, (1 - section) * half, half, 0)
    return (mine.astype(F32) + swap(other, "section", 1).astype(F32)).astype(BF)


def dp_sum(arrays, turn):
    order = list(range(lax.axis_size("dp")))
    order = order[turn:] + order[:turn]
    return lax.psum(arrays, "dp", axis_index_groups=[order])


def plus(left, right):
    return (left.astype(F32) + right.astype(F32)).astype(BF)


def sum_over(array, axes):
    for axis in axes:
        bit = 1
        while bit < lax.axis_size(axis):
            array = array + swap(array, axis, bit)
            bit *= 2
    return array


def shards(
    token_ids,
    targets,
    lengths,
    embedding,
    w_qkv,
    b_qv,
    w_out,
    w_in,
    b_in,
    w_down,
    norm_gains,
    shifts,
    mask_logits,
    mask_noise,
):
    section = lax.axis_index("section")
    first = section == 0
    place = lax.axis_index("tensor")
    me = place[None].astype(jnp.int32)
    tokens = token_ids.shape[1]
    rows = tokens // lax.axis_size("tensor")
    width = embedding.shape[1]
    vocab_rows = embedding.shape[0]
    vocab_start = place * vocab_rows
    head_width = w_qkv.shape[3]
    order = place ^ jnp.arange(4, dtype=jnp.int32)

    gate_own = jax.nn.sigmoid(mask_logits[0] + mask_noise[0])
    small = jnp.concatenate(
        [
            norm_gains[0],
            shifts[0],
            b_in[0][None],
            jnp.pad(b_qv[0], ((0, 0), (0, width - head_width))),
        ]
    )
    held = (w_qkv[0].reshape(width, 3 * head_width), w_out[0], w_in[0], w_down[0], small, gate_own)
    brought = jax.tree.map(lambda a: swap(a, "section", 1), held)

    def weights_of(layer):
        kept = section == layer
        wq, wo, wi, wd, vec, gates = jax.tree.map(lambda a, b: jnp.where(kept, a, b), held, brought)
        bias = jnp.concatenate(
            [
                vec[7:8, :PART],
                jnp.zeros((1, PART), F32),
                vec[8:9, :PART],
            ],
            axis=1,
        )
        wq = pad_parts(wq.reshape(width, 3, head_width), 2).reshape(width, 3 * PART)
        return (wq, bias, pad_parts(wo, 0), wi, vec[6:7], wd, vec[0:2], vec[2:6], gates)

    layers = [weights_of(0), weights_of(1)]
    lens = lax.dynamic_index_in_dim(lengths, section, 0, keepdims=False)

    def mine(ids):
        row = lax.dynamic_index_in_dim(ids, section, 0, keepdims=False)
        return row.reshape(4, rows)[order].reshape(tokens) - vocab_start

    target_local, token_local = mine(targets), mine(token_ids)
    x = lookup_rows(token_local, embedding).astype(F32) * width**0.5
    target_rows = lookup_rows(target_local, embedding)
    hidden, hidden_low, saved_first = layer_forward(x, x.astype(BF), lens, me, layers[0])
    final, final_low, saved_last = layer_forward(hidden, hidden_low, lens, me, layers[1])

    dp = lax.axis_size("dp")
    pieces = gather_pieces(final_low)
    rows_of = [final_low] + [swap(final_low, "dp", other) for other in range(1, dp)]
    (own,) = head_blocks(pieces[:1], embedding, [(rows, F32)])
    own, *pieces[1:] = lax.optimization_barrier((own, *pieces[1:]))
    near, far, corner = head_blocks(pieces[1:], embedding, [(rows, BF)] * 3)
    there = [pieces] + [gather_pieces(r) for r in rows_of[1:]]
    near, far, corner, there[1:2] = lax.optimization_barrier((near, far, corner, there[1:2]))
    near, far, corner = swap(near, "tensor", 1), swap(far, "tensor", 2), swap(corner, "tensor", 3)
    outs = [sds((rows, width), F32), sds((rows, width), BF), sds((8, width), F32), sds((8, rows), F32)]
    d_two, d_two_low, sums_two_last, spread = kernel_call(
        merge_head,
        "merge_head",
        outs,
        [],
        [own, near, far, corner, target_rows, saved_last[8], saved_last[9], layers[1][6][1:2]],
    )
    d_pieces = gather_pieces(d_two_low)

    half_vocab = vocab_rows // 2
    share = half_vocab // dp
    steps = 2 if (share // 2) % 16 == 0 else 1
    starts = [lax.axis_index("dp") * share + c * half_vocab for c in (section, 1 - section)]
    firsts = [(start + jnp.arange(0, share, share // steps, dtype=jnp.int32)).astype(jnp.int32) for start in starts]
    my_rows = [lax.dynamic_slice_in_dim(embedding, start, share, 0) for start in starts]
    spread = jnp.concatenate([spread[0:1]] + [swap(spread, "tensor", bit)[0:1] for bit in (1, 2, 3)], axis=1)
    d_rows = [jnp.zeros((share, width), F32)] * 2
    id_pair = jnp.stack([token_local, target_local])
    id_pairs = [id_pair] + [swap(id_pair, "dp", other) for other in range(1, dp)]
    spreads = [spread] + [swap(spread, "dp", other) for other in range(1, dp)]

    def dense_half(values, half):
        total = d_rows[half]
        for others in groups(4):
            found = sum([there[other] for other in others], [])
            columns = [jnp.concatenate([spreads[other] for other in others], axis=1)]
            columns += [jnp.concatenate([id_pairs[other][1:2] for other in others], axis=1)]
            total = owned_rows(vocab_backward, "vocab_backward", found, columns, firsts[half], total, my_rows[half])
        values, d_rows[half] = lax.optimization_barrier((values, total))
        return values

    def groups(size):
        return [range(at, min(at + size, dp)) for at in range(0, dp, size)]

    sums = []

    def early_sum(d_feed, turn):
        sums.append(dp_sum(d_feed, turn))

    def held(values, k):
        values, sums[k] = lax.optimization_barrier((values, sums[k]))
        return values

    d_x, d_rest_last, vecs_last = layer_backward(
        d_two,
        d_pieces,
        lens,
        me,
        layers[1],
        saved_last,
        section,
        head_width,
        [lambda v: v] * 3,
    )
    outs = [sds((rows, width), F32), sds((rows, width), F32), sds((rows, width), BF), sds((8, width), F32)]
    grad_last, d_two, d_two_low, sums_two_first = kernel_call(
        norm_backward,
        "second_norm_grad",
        outs,
        [],
        list(d_x) + [saved_first[8], saved_first[9], layers[0][6][1:2]],
    )
    d_pieces, d_rest_last, there[1:] = lax.optimization_barrier((gather_pieces(d_two_low), d_rest_last, there[1:]))
    early_sum(d_rest_last, 0)
    d_x, d_rest_first, vecs_first = layer_backward(
        d_two,
        d_pieces,
        lens,
        me,
        layers[0],
        saved_first,
        section,
        head_width,
        [lambda v: v, lambda v: v, lambda v: held(dense_half(v, 1), 0)],
    )
    def vec_rows(vecs, sums_two):
        d_b_qkv, d_b_in, sums_one = vecs
        wide = jnp.concatenate([sums_one[0:1], sums_two[0:1], sums_one[2:3], sums_one[1:2], sums_two[2:3], sums_two[1:2]])
        narrow = jnp.concatenate(
            [jnp.pad(d_b_qkv[:, :PART], ((0, 0), (0, width - PART))), jnp.pad(d_b_qkv[:, 2 * PART :], ((0, 0), (0, width - PART))), d_b_in]
        )
        spread_out = jnp.where((jnp.arange(4) == place)[:, None, None], narrow[None], 0.0).reshape(12, width)
        return jnp.concatenate([wide, spread_out])

    vecs = jnp.stack([vec_rows(vecs_first, sums_two_first), vec_rows(vecs_last, sums_two_last)])
    vecs = sum_over(vecs, ("tensor", "section")).astype(BF).reshape(-1, width)
    d_feed_first, d_attn, d_gate = d_rest_first
    d_x, d_feed_first, d_attn, d_gate, vecs = lax.optimization_barrier((d_x, d_feed_first, d_attn, d_gate, vecs))
    early_sum((d_feed_first, jnp.concatenate([d_attn, vecs]), d_gate), 1)
    grad_first = d_x[3] + (d_x[0] + d_x[1].astype(F32) + d_x[2].astype(F32))

    rows_here = grad_first.astype(BF)
    arriving = [swap(rows_here, "dp", other) for other in range(1, dp)]
    own_pieces, arriving = dense_half((gather_pieces(rows_here), arriving), 0)
    found = [own_pieces] + [gather_pieces(r) for r in arriving]
    for others in groups(3):
        ids = jnp.concatenate([id_pairs[other][0:1] for other in others], axis=1)
        pieces = sum([found[other] for other in others], [])
        d_rows = [
            owned_rows(embed_backward, "embed_backward", pieces, [ids], *part)
            for part in reversed(list(zip(firsts, d_rows)))
        ][::-1]
    d_embedding = d_rows[0] + swap(d_rows[1].astype(BF), "section", 1).astype(F32)

    def assembled(low_layer, high_layer):
        got = swap(jnp.where(first, high_layer, low_layer), "section", 1)
        return jnp.where(first, low_layer, got).astype(F32), jnp.where(first, got, high_layer).astype(F32)

    grads_last, (d_feed, d_attn, d_gate) = sums
    grads_first = (d_feed, d_attn[: width // 2], d_gate)
    vecs = d_attn[width // 2 :].reshape(2, -1, width)
    vecs = lax.dynamic_index_in_dim(vecs, section, 0, keepdims=False).astype(F32)
    narrow = lax.dynamic_slice_in_dim(vecs, 6 + 3 * place, 3, 0)
    (g_in, g_down), attn, gate = jax.tree.map(assembled, grads_first, grads_last)
    attn = jnp.concatenate(attn)
    g_qkv = attn[:, : 3 * head_width].reshape(width, 3, head_width)
    g_out = attn[:, 3 * head_width :].T
    g_mask = jnp.concatenate(gate).reshape(gate_own.shape) * gate_own * (1.0 - gate_own)

    def placed_rows(low_layer, high_layer):
        got = swap(jnp.where(first, high_layer, low_layer), "section", 1)
        return jnp.where(first, jnp.stack([low_layer, got]), jnp.stack([got, high_layer]))

    return (
        placed_rows(hidden, final)[None],
        placed_rows(grad_first, grad_last)[None],
        d_embedding,
        g_qkv[None],
        narrow[None, 0:2, :head_width],
        g_out[None],
        g_in[None],
        narrow[None, 2],
        g_down[None],
        vecs[None, 0:2],
        vecs[None, 2:6],
        g_mask[None],
    )


def solution(mesh):
    placed = (
        P("dp", None),
        P("dp", None),
        P("dp", None),
        P("tensor", None),
        P("section", None, None, "tensor"),
        P("section", None, "tensor"),
        P("section", "tensor", None),
        P("section", None, "tensor"),
        P("section", "tensor"),
        P("section", "tensor", None),
        P("section", None, None),
        P("section", None, None),
        P("section", "tensor", None, None),
        P("section", "tensor", None, None),
    )
    return jax.shard_map(
        shards,
        mesh=mesh,
        in_specs=placed,
        out_specs=(
            P("section", "dp", "tensor", None),
            P("section", "dp", "tensor", None),
            P(("tensor", "section", "dp"), None),
            P("section", None, None, "tensor"),
            P("section", None, "tensor"),
            P("section", "tensor", None),
            P("section", None, "tensor"),
            P("section", "tensor"),
            P("section", "tensor", None),
            P("section", None, None),
            P("section", None, None),
            P("section", "tensor", None, None),
        ),
        check_vma=False,
    )
```
